128 devices in a mesh: row: 8 (over z, core), col: 16 (over x, y).
Axes of the slice: x: 4, y: 4, z: 4, core: 2. Of those that a mesh axis runs over, the one named last changes fastest.
Arguments:
- front_block: bfloat16 [24576, 16384], P('row', 'col'), may hold values from -6 to 246, as said below
- child_blocks: bfloat16 [2, 16384, 8192], P(None, 'row', 'col'), may hold values from -6 to 6
- row_offsets: int32 [2, 16384], replicated, may hold values from -1 to 127, as said below
- tile_targets: int32 [2, 128], replicated, may hold values from 0 to 191, as said below
Outputs:
- factored: float32 [24576, 16384], P('row', 'col')
The draws below stay inside these ranges and needn't reach their ends.
Inputs may be any that keep to these rules, and one draw needn't show every extreme that they name: `front_block`: entries on the front's natural diagonal lie between 114 and 246, the others between -6 and 6. `row_offsets`: within each tile of 128 child indices the entries that are not -1 are distinct and come first; each tile holds 64 or more of them. `tile_targets`: A child's tiles go to distinct front tiles; tile t goes to a front tile below 128 exactly when t < 64. Among one child's tiles with equal t % 8, exactly 2 go to front tiles of each value of tile % 8. Among the tiles t < 64 of both children with equal t % 16, at most 1 go to front tiles of one value of tile % 16, and 1 do for some value. Every value of tile % 16 receives the same number of a child's tiles t < 64, and every value of tile % 8 the same number of a child's tiles.
All inputs are finite; a program needn't handle non-finite values.
Results may differ from the reference program's by a relative error of at most 0.0017.
Values may be sent and summed in bfloat16 or wider, within the bound.
A program may use at most 192 MiB of HBM per device.

```python
import jax
import jax.numpy as jnp
from jax import lax

TILE = 128
FRONT = 24576
WINDOW = 16384
CHILD = 16384
CHILD_COLS = 8192
PANEL = 256
PANELS = 2
GRID_ROWS = 8
GRID_COLS = 16


def draw_front_block(key, part):
    key = jax.random.fold_in(key, 11)
    key_one, key_two, key_three, key_four = jax.random.split(key, 4)
    values = jax.random.truncated_normal(key_one, -6.0, 6.0, (FRONT, WINDOW), jnp.float32)
    magnitude = jax.random.uniform(key_three, (FRONT, WINDOW), jnp.float32, 2.0, 6.0)
    row_ids = jnp.arange(FRONT)
    col_ids = jnp.arange(WINDOW)
    row_span = FRONT // GRID_ROWS
    col_span = WINDOW // GRID_COLS
    nat_rows = (row_ids % row_span // TILE * GRID_ROWS + row_ids // row_span) * TILE + row_ids % TILE
    nat_cols = (col_ids % col_span // TILE * GRID_COLS + col_ids // col_span) * TILE + col_ids % TILE
    signs = jnp.where(jax.random.randint(key_four, (FRONT,), 0, 2) == 1, 1.0, -1.0).astype(jnp.float32)
    pattern = signs[nat_rows][:, None] * signs[nat_cols][None, :]
    same_panel = nat_rows[:, None] // PANEL == nat_cols[None, :] // PANEL
    in_pivot = same_panel & (nat_rows[:, None] < PANELS * PANEL)
    values = jnp.where(in_pivot, pattern * magnitude, values)
    boosts = jax.random.uniform(key_two, (FRONT,), jnp.float32, 120.0, 240.0)
    return jnp.where(nat_rows[:, None] == nat_cols[None, :], values + boosts[:, None], values).astype(jnp.bfloat16)


def draw_row_offsets(key, part):
    key = jax.random.fold_in(key, 7)
    key_one, key_two = jax.random.split(key)
    tile_count = 2 * (CHILD // TILE)
    shuffles = jax.vmap(lambda k: jax.random.permutation(k, TILE))(jax.random.split(key_one, tile_count))
    live_rows = jax.random.randint(key_two, (tile_count, 1), TILE // 2, TILE + 1)
    offsets = jnp.where(jnp.arange(TILE)[None, :] < live_rows, shuffles, -1)
    return offsets.reshape(2, CHILD).astype(jnp.int32)


def grid_shifts(key):
    key_one, key_two = jax.random.split(key)
    ordering = jnp.concatenate([jnp.arange(2, dtype=jnp.int32), 2 + jax.random.permutation(key_one, GRID_ROWS - 2).astype(jnp.int32)])
    flip_bits = jax.random.randint(key_two, (GRID_ROWS,), 0, 2)
    flip_bits = jnp.where(jnp.arange(GRID_ROWS) < 2, 0, flip_bits)
    residue_ids = jnp.arange(GRID_COLS)
    upper_bit = jnp.where(residue_ids < GRID_ROWS, flip_bits[residue_ids % GRID_ROWS], 1 - flip_bits[residue_ids % GRID_ROWS])
    return (ordering[residue_ids % GRID_ROWS] + GRID_ROWS * upper_bit).astype(jnp.int32)


def ranks_within(classes, count_each, length):
    ordering = jnp.argsort(classes * length + jnp.arange(length), stable=True)
    position = jnp.zeros((length,), jnp.int32).at[ordering].set(jnp.arange(length, dtype=jnp.int32))
    return position - classes * count_each


def level_tables(key, count_rows, width):
    return jax.vmap(lambda k: jax.random.permutation(k, width))(jax.random.split(key, count_rows))


def child_targets(key, shifts, child_index):
    tile_count = CHILD // TILE
    narrow = CHILD_COLS // TILE
    window_tiles = WINDOW // TILE
    per_col = narrow // GRID_COLS
    rest_count = tile_count - narrow
    per_row = rest_count // GRID_ROWS
    subkeys = jax.random.split(key, 3)
    tile_ids = jnp.arange(narrow)
    shift_of = shifts[(child_index * per_col + tile_ids // GRID_COLS) % GRID_COLS]
    classes = (tile_ids % GRID_COLS + shift_of) % GRID_COLS
    ranking = ranks_within(classes, per_col, narrow)
    levels = level_tables(subkeys[0], GRID_COLS, window_tiles // GRID_COLS)
    dest_wide = levels[classes, ranking] * GRID_COLS + classes
    residues = shifts[(child_index * per_col + jnp.arange(per_col)) % GRID_COLS] % GRID_ROWS
    tallies = jnp.sum(residues[:, None] == jnp.arange(GRID_ROWS)[None, :], axis=0)
    needed = tile_count // (GRID_ROWS * GRID_ROWS) - 2 * tallies
    limits = jnp.cumsum(needed)
    steps_of = jnp.searchsorted(limits, jnp.arange(per_row), side='right')
    shuffle = level_tables(subkeys[1], GRID_ROWS, per_row)
    moves_of = steps_of[shuffle]
    owners = (jnp.arange(GRID_ROWS)[:, None] + moves_of) % GRID_ROWS
    flat_owner = owners.T.reshape(rest_count).astype(jnp.int32)
    ranking_rest = ranks_within(flat_owner, per_row, rest_count)
    levels_rest = level_tables(subkeys[2], GRID_ROWS, per_row)
    dest_rest = window_tiles + levels_rest[flat_owner, ranking_rest] * GRID_ROWS + flat_owner
    return jnp.concatenate([dest_wide, dest_rest]).astype(jnp.int32)


def draw_tile_targets(key, part):
    key = jax.random.fold_in(key, 5)
    key_shift, key_one, key_two = jax.random.split(key, 3)
    shifts = grid_shifts(key_shift)
    return jnp.stack([child_targets(key_one, shifts, 0), child_targets(key_two, shifts, 1)])


def shard_levels(own_key, dims, cuts, smallest, top_value):
    def one(dim, blocks):
        steps = jax.random.uniform(jax.random.fold_in(jax.random.fold_in(own_key, 6), dim), (blocks,), jnp.float32, smallest / len(cuts), top_value / len(cuts))
        return jnp.repeat(jnp.exp(steps), dims[dim] // blocks).reshape((-1,) + (1,) * (len(dims) - dim - 1))

    gain = one(*cuts[0])
    for cut in cuts[1:]:
        gain = gain * one(*cut)
    return gain


def normal_values(own_key, dims, scale, limit, cuts=(), kind=jnp.bfloat16):
    level = shard_levels(own_key, dims, cuts, -0.22, 0.18) if cuts else 1.0
    entries = jax.random.normal(own_key, dims, jnp.float32) * scale * level
    return jnp.minimum(jnp.maximum(entries, -limit), limit).astype(kind)


def setup_inputs(seed: int = 0) -> dict:
    splits = jax.random.split(jax.random.key(seed), 5)
    front_block = draw_front_block(jax.random.fold_in(splits[4], 71), 0)
    child_blocks = normal_values(splits[1], (2, CHILD, CHILD_COLS), 1.0, 6.0, ((1, 8), (2, 16)))
    row_offsets = draw_row_offsets(jax.random.fold_in(splits[4], 71), 0)
    tile_targets = draw_tile_targets(jax.random.fold_in(splits[4], 71), 0)
    return dict(front_block=front_block, child_blocks=child_blocks, row_offsets=row_offsets, tile_targets=tile_targets)


def to_natural(stored, rows_total, cols_total):
    shaped = stored.reshape(GRID_ROWS, rows_total // (TILE * GRID_ROWS), TILE, GRID_COLS, cols_total // (TILE * GRID_COLS), TILE)
    return shaped.transpose(1, 0, 2, 4, 3, 5).reshape(rows_total, cols_total)

def to_storage(natural, rows_total, cols_total):
    shaped = natural.reshape(rows_total // (TILE * GRID_ROWS), GRID_ROWS, TILE, cols_total // (TILE * GRID_COLS), GRID_COLS, TILE)
    return shaped.transpose(1, 0, 2, 4, 3, 5).reshape(rows_total, cols_total)

def scatter_child(working, child_block, targets, col_targets):

    def add_tile(index, current):
        begin_row = index * TILE
        row_targets = lax.dynamic_slice_in_dim(targets, begin_row, TILE)
        block_rows = lax.dynamic_slice_in_dim(child_block, begin_row, TILE, 0).astype(jnp.float32)
        return current.at[row_targets[:, None], col_targets[None, :]].add(block_rows, mode='drop')
    return lax.fori_loop(0, CHILD // TILE, add_tile, working)

def reference(front_block, child_blocks, row_offsets, tile_targets):
    working = to_natural(front_block, FRONT, WINDOW).astype(jnp.float32)
    for child_index in range(2):
        child_block = to_natural(child_blocks[child_index], CHILD, CHILD_COLS)
        targets = tile_targets[child_index][jnp.arange(CHILD) // TILE] * TILE + row_offsets[child_index]
        targets = jnp.where(row_offsets[child_index] >= 0, targets, FRONT).astype(jnp.int32)
        working = scatter_child(working, child_block, targets, targets[:CHILD_COLS])
    height = 16 * TILE
    for panel_index in range(PANELS):
        begin_col = panel_index * PANEL
        finish = begin_col + PANEL
        pivot_block = jnp.linalg.cholesky(working[begin_col:finish, begin_col:finish])
        below_rows = lax.linalg.triangular_solve(pivot_block, working[finish:, begin_col:finish], left_side=False, lower=True, transpose_a=True)
        for top_row in range(finish, FRONT, height):
            bottom_row = min(top_row + height, FRONT)
            product = jnp.dot(below_rows[top_row - finish:bottom_row - finish].astype(jnp.float32), below_rows[:WINDOW - finish].T.astype(jnp.float32), precision=lax.Precision.HIGHEST, preferred_element_type=jnp.float32)
            working = working.at[top_row:bottom_row, finish:].add(-product)
        column = jnp.concatenate([jnp.zeros((begin_col, PANEL), jnp.float32), pivot_block, below_rows], axis=0)
        working = working.at[:, begin_col:finish].set(column)
    return to_storage(working, FRONT, WINDOW)
```

```python
import jax
import jax.numpy as jnp
from jax import lax
from jax.experimental import pallas as pl
from jax.experimental.pallas import tpu as pltpu
from jax.sharding import PartitionSpec as P

TILE = 128
ROWS = 8
COLS = 16
DEVICES = ROWS * COLS
MESH = pl.DeviceIdType.MESH
VMEM_LIMIT = 56 * 2**20
BF16 = jnp.bfloat16
F32 = jnp.float32
NT = (((1,), (1,)), ((), ()))


def spec(space):
    return pl.BlockSpec(memory_space=space)


def iota(dim):
    return lax.broadcasted_iota(jnp.int32, (TILE, TILE), dim)


def one_hot(offsets):
    return jnp.where(iota(0) == offsets, 1.0, 0.0).astype(BF16)


def place_kernel(targets, where, offsets, child, front, picked, corner, shifted, rank, seen):
    p = where[0]
    q = where[1]
    corner[...] = jnp.zeros_like(corner)

    @pl.when((p < 4) & (q < 4))
    def _():
        corner[p * 4 + q] = front[...].astype(F32)

    for c in range(2):
        for d in range(ROWS):
            seen[d] = 0

        def order(l, carry):
            owner = lax.rem(targets[c, l * ROWS + p], ROWS)
            rank[l] = owner * COLS * 2 + seen[owner]
            seen[owner] = seen[owner] + 1
            return carry

        lax.fori_loop(0, 16, order, 0)

        def shift(l, carry):
            hot = one_hot(offsets[c, pl.ds(l * ROWS + p, 1), :])
            at = pl.ds(pl.multiple_of(l * TILE, TILE), TILE)
            moved = jnp.dot(hot, child[c, at, :], preferred_element_type=F32)
            shifted[at, :] = moved.astype(BF16)
            return carry

        lax.fori_loop(0, 16, shift, 0, unroll=4)
        for k in range(4):
            hot = one_hot(offsets[c, pl.ds(k * COLS + q, 1), :])
            front_col = targets[c, k * COLS + q]
            base = lax.rem(front_col, COLS) * 2
            for part in range(4):
                rows = shifted[part * 512 : (part + 1) * 512, k * TILE : (k + 1) * TILE]
                placed = lax.dot_general(rows, hot, NT, preferred_element_type=F32)
                for s in range(4):
                    l = part * 4 + s
                    tile = placed[s * TILE : (s + 1) * TILE]
                    picked[rank[l] + base] = tile.astype(BF16)
                    front_row = targets[c, l * ROWS + p]

                    @pl.when((front_row < 4) & (front_col < 4))
                    def _(tile=tile, front_row=front_row, front_col=front_col):
                        corner[front_row * 4 + front_col] += tile


def place(targets, where, offsets, child, front):
    return pl.pallas_call(
        place_kernel,
        out_shape=(
            jax.ShapeDtypeStruct((DEVICES * 2, TILE, TILE), BF16),
            jax.ShapeDtypeStruct((16, TILE, TILE), F32),
        ),
        in_specs=[spec(pltpu.SMEM), spec(pltpu.SMEM)] + [spec(pltpu.VMEM)] * 3,
        out_specs=(spec(pltpu.VMEM), spec(pltpu.VMEM)),
        scratch_shapes=[
            pltpu.VMEM((16 * TILE, 4 * TILE), BF16),
            pltpu.SMEM((16,), jnp.int32),
            pltpu.SMEM((ROWS,), jnp.int32),
        ],
        compiler_params=pltpu.CompilerParams(vmem_limit_bytes=VMEM_LIMIT),
        cost_estimate=pl.CostEstimate(flops=2**31, bytes_accessed=14 * 2**20, transcendentals=0),
        name="place",
    )(targets, where, offsets, child, front)


def corner_kernel(part, whole, held, send, recv, send_sum, recv_sum, local):
    p = lax.axis_index("row")
    q = lax.axis_index("col")
    me = p * COLS + q
    barrier = pltpu.get_barrier_semaphore()

    def greet(d, carry):
        t = lax.rem(me + d, DEVICES)
        pl.semaphore_signal(
            barrier, inc=1, device_id=(t // COLS, lax.rem(t, COLS)), device_id_type=MESH
        )
        return carry

    lax.fori_loop(1, DEVICES, greet, 0)
    pl.semaphore_wait(barrier, DEVICES - 1)
    own = pltpu.make_async_copy(part.at[me], held.at[me], local)
    own.start()

    def scatter(d, carry):
        t = lax.rem(me + d, DEVICES)
        pltpu.make_async_remote_copy(
            part.at[t],
            held.at[me],
            send,
            recv,
            device_id=(t // COLS, lax.rem(t, COLS)),
            device_id_type=MESH,
        ).start()
        return carry

    lax.fori_loop(1, DEVICES, scatter, 0)
    own.wait()
    others = pl.ds(0, DEVICES - 1)
    pltpu.make_async_copy(held.at[others], held.at[others], recv).wait()
    whole[me] = jnp.sum(held[...], axis=0)

    def gather(d, carry):
        t = lax.rem(me + d, DEVICES)
        pltpu.make_async_remote_copy(
            whole.at[me],
            whole.at[me],
            send_sum,
            recv_sum,
            device_id=(t // COLS, lax.rem(t, COLS)),
            device_id_type=MESH,
        ).start()
        return carry

    lax.fori_loop(1, DEVICES, gather, 0)
    pltpu.make_async_copy(part.at[others], part.at[others], send).wait()
    pltpu.make_async_copy(whole.at[others], whole.at[others], send_sum).wait()
    pltpu.make_async_copy(whole.at[others], whole.at[others], recv_sum).wait()


def sum_corner(part):
    return pl.pallas_call(
        corner_kernel,
        out_shape=jax.ShapeDtypeStruct((DEVICES, 16, TILE), F32),
        in_specs=[spec(pltpu.VMEM)],
        out_specs=spec(pltpu.VMEM),
        scratch_shapes=[pltpu.VMEM((DEVICES, 16, TILE), F32)] + [pltpu.SemaphoreType.DMA] * 5,
        compiler_params=pltpu.CompilerParams(
            collective_id=1, has_side_effects=True, vmem_limit_bytes=VMEM_LIMIT
        ),
        cost_estimate=pl.CostEstimate(flops=2**18, bytes_accessed=2**22, transcendentals=0),
        name="corner",
    )(part)


def mm(a, b):
    return jnp.dot(a, b, precision=lax.Precision.HIGHEST, preferred_element_type=F32)


def mm_nt(a, b):
    return lax.dot_general(
        a, b, NT, precision=lax.Precision.HIGHEST, preferred_element_type=F32
    )


def factor_tile(a):
    blocks = TILE // 8
    sub = lax.broadcasted_iota(jnp.int32, (8, 1), 0)
    eye = jnp.where(iota(0) == iota(1), 1.0, 0.0)
    upper = [a[i * 8 : (i + 1) * 8] for i in range(blocks)]
    inverse = [eye[i * 8 : (i + 1) * 8] for i in range(blocks)]
    for s in range(TILE):
        b, r = s // 8, s % 8
        u_row = upper[b][r : r + 1]
        i_row = inverse[b][r : r + 1]
        scale = 1.0 / u_row[:, s : s + 1]
        u_row = u_row * scale
        i_row = i_row * scale
        for i in range(b, blocks):
            column = upper[i][:, s : s + 1]
            if i == b:
                if r == 7:
                    continue
                column = jnp.where(sub > r, column, 0.0)
            upper[i] = upper[i] - column * u_row
            inverse[i] = inverse[i] - column * i_row
    u = jnp.concatenate(upper, axis=0)
    inv = jnp.concatenate(inverse, axis=0)
    diagonal = jnp.sum(jnp.where(iota(0) == iota(1), u, 0.0), axis=1, keepdims=True)
    root = lax.rsqrt(diagonal)
    u = jnp.where(iota(1) >= iota(0), u * root, 0.0)
    return u.T, inv * root


def factor_kernel(corner, lower, inverse, work, inv):
    def symmetric(i, j):
        return (corner[i * 4 + j] + corner[j * 4 + i].T) * 0.5

    for i in range(4):
        for j in range(i + 1):
            work[i * 4 + j] = symmetric(i, j) if i // 2 == j // 2 else corner[i * 4 + j]
    lower[...] = jnp.zeros_like(lower)

    def panel(j, carry):
        pivot, pivot_inv = factor_tile(work[j * 5])
        lower[j * 5] = pivot
        inv[j * 5] = pivot_inv

        def solve(i, carry):
            lower[i * 4 + j] = mm_nt(work[i * 4 + j], pivot_inv)
            return carry

        lax.fori_loop(j + 1, 4, solve, 0)

        def update_row(i, carry):
            def update(k, carry):
                work[i * 4 + k] -= mm_nt(lower[i * 4 + j], lower[k * 4 + j])
                return carry

            return lax.fori_loop(j + 1, i + 1, update, carry)

        lax.fori_loop(j + 1, 4, update_row, 0)
        return carry

    lax.fori_loop(0, 4, panel, 0)
    inverse[...] = jnp.zeros_like(inverse)
    for j in range(4):
        column = {j: inv[j * 5]}
        for i in range(j + 1, 4):
            total = mm(lower[i * 4 + j], column[j])
            for k in range(j + 1, i):
                total = total + mm(lower[i * 4 + k], column[k])
            column[i] = -mm(inv[i * 5], total)
        for i in range(j, 4):
            inverse[i * TILE : (i + 1) * TILE, j * TILE : (j + 1) * TILE] = column[i].astype(BF16)


def factor(corner):
    return pl.pallas_call(
        factor_kernel,
        out_shape=(
            jax.ShapeDtypeStruct((16, TILE, TILE), F32),
            jax.ShapeDtypeStruct((4 * TILE, 4 * TILE), BF16),
        ),
        in_specs=[spec(pltpu.VMEM)],
        out_specs=(spec(pltpu.VMEM), spec(pltpu.VMEM)),
        scratch_shapes=[pltpu.VMEM((16, TILE, TILE), F32), pltpu.VMEM((16, TILE, TILE), F32)],
        compiler_params=pltpu.CompilerParams(vmem_limit_bytes=VMEM_LIMIT),
        cost_estimate=pl.CostEstimate(flops=2**30, bytes_accessed=2**22, transcendentals=0),
        name="factor",
    )(corner)


def index_rows(targets, p, row_from, seen):
    def clear(i, carry):
        row_from[i] = -1
        return carry

    lax.fori_loop(0, 48, clear, 0)
    for c in range(2):
        for d in range(ROWS):
            seen[d] = 0

        def visit(t, carry):
            goal = targets[c, t]

            @pl.when(lax.rem(goal, ROWS) == p)
            def _():
                source = lax.rem(t, ROWS)
                row_from[c * 24 + goal // ROWS] = source * COLS * 2 + seen[source]
                seen[source] = seen[source] + 1

            return carry

        lax.fori_loop(0, 128, visit, 0)


def index_cols(targets, q, col_from):
    for i in range(16):
        col_from[i] = -1
    for c in range(2):

        def visit(t, carry):
            goal = targets[c, t]

            @pl.when(lax.rem(goal, COLS) == q)
            def _():
                col_from[c * 8 + goal // COLS] = lax.rem(t, COLS) * 2

            return carry

        lax.fori_loop(0, 64, visit, 0)


def column_kernel(targets, where, front, arrived, column, total, row_from, col_from, seen):
    p = where[0]
    q = where[1]

    @pl.when(q < 4)
    def _():
        index_rows(targets, p, row_from, seen)
        index_cols(targets, q, col_from)

        def tile(l, carry):
            total[...] = front[pl.ds(pl.multiple_of(l * TILE, TILE), TILE), :].astype(F32)
            for c in range(2):
                row, col = row_from[c * 24 + l], col_from[c * 8]

                @pl.when((row >= 0) & (col >= 0))
                def _(row=row, col=col):
                    total[...] += arrived[row + col].astype(F32)

            column[l] = total[...].astype(BF16)
            return carry

        lax.fori_loop(0, 24, tile, 0)


def first_column(targets, where, front, arrived):
    return pl.pallas_call(
        column_kernel,
        out_shape=jax.ShapeDtypeStruct((24, TILE, TILE), BF16),
        grid=(1,),
        in_specs=[
            spec(pltpu.SMEM),
            spec(pltpu.SMEM),
            pl.BlockSpec((24 * TILE, TILE), lambda i: (0, 0)),
            pl.BlockSpec((DEVICES * 2, TILE, TILE), lambda i: (0, 0, 0)),
        ],
        out_specs=pl.BlockSpec((24, TILE, TILE), lambda i: (0, 0, 0)),
        scratch_shapes=[
            pltpu.VMEM((TILE, TILE), F32),
            pltpu.SMEM((48,), jnp.int32),
            pltpu.SMEM((16,), jnp.int32),
            pltpu.SMEM((ROWS,), jnp.int32),
        ],
        compiler_params=pltpu.CompilerParams(vmem_limit_bytes=VMEM_LIMIT),
        cost_estimate=pl.CostEstimate(flops=2**20, bytes_accessed=2**23, transcendentals=0),
        name="column",
    )(targets, where, front, arrived)


def spread_kernel(column, rows, cols, sends, recvs, local):
    p = lax.axis_index("row")
    q = lax.axis_index("col")
    z, core = p // 2, lax.rem(p, 2)
    x, y = q // 4, lax.rem(q, 4)

    def at_x(d):
        return (p, lax.rem(x + d, 4) * 4 + y)

    def at_y(d):
        return (p, x * 4 + lax.rem(y + d, 4))

    def at_z(d):
        return (lax.rem(z + d, 4) * 2 + core, q)

    sibling = (z * 2 + 1 - core, q)
    barrier = pltpu.get_barrier_semaphore()
    for d in (1, 2, 3):
        for peer in (at_x(d), at_y(d), at_z(d)):
            pl.semaphore_signal(barrier, inc=1, device_id=peer, device_id_type=MESH)
    pl.semaphore_signal(barrier, inc=1, device_id=sibling, device_id_type=MESH)
    pl.semaphore_wait(barrier, 10)

    def copy(src, dst, slot, peer):
        return pltpu.make_async_remote_copy(
            src, dst, sends.at[slot], recvs.at[slot], device_id=peer, device_id_type=MESH
        )

    def quarter(owner_x):
        return rows.at[y, owner_x]

    @pl.when(x == 0)
    def _():
        out = [copy(column.at[d], rows.at[y, d], d - 1, at_x(d)) for d in (1, 2, 3)]
        for one in out:
            one.start()
        own = pltpu.make_async_copy(column.at[0], rows.at[y, 0], local)
        own.start()
        own.wait()
        for one in out:
            one.wait_send()

    for d in (1, 2, 3):

        @pl.when(x == d)
        def _(d=d):
            copy(column.at[d], rows.at[y, d], d - 1, at_x(4 - d)).wait_recv()

    first = []
    for d in (1, 2, 3):
        half = rows.at[y, x, 0]
        first.append(copy(half, half, 2 + d, at_x(d)))
        half = rows.at[y, x, 1]
        first.append(copy(half, half, 5 + d, at_y(d)))
    for one in first:
        one.start()
    for one in first:
        one.wait()
    second = []
    for d in (1, 2, 3):
        half = rows.at[y, :, 0]
        second.append(copy(half, half, 8 + d, at_y(d)))
        half = rows.at[:, x, 1]
        second.append(copy(half, half, 11 + d, at_x(d)))
    for one in second:
        one.start()
    for one in second:
        one.wait()

    source = lax.rem(q, ROWS)
    lead = source // 2
    for m in range(8):
        l = 2 * m + q // ROWS
        tile = rows.at[:, l // 6, lax.rem(l, 6) // 3, lax.rem(l, 3)]

        @pl.when(p == source)
        def _(m=m, tile=tile):
            own = pltpu.make_async_copy(tile, cols.at[m], local)
            own.start()
            own.wait()

    @pl.when(p == source)
    def _():
        out = [copy(cols, cols, 14 + d, at_z(d)) for d in (1, 2, 3)]
        out.append(copy(cols, cols, 18, sibling))
        for one in out:
            one.start()
        for one in out:
            one.wait_send()

    for d in (1, 2, 3):

        @pl.when((core == lax.rem(source, 2)) & (lax.rem(lead + d, 4) == z))
        def _(d=d):
            copy(cols, cols, 14 + d, at_z(4 - d)).wait_recv()
            on = copy(cols, cols, 18, sibling)
            on.start()
            on.wait_send()

    @pl.when(core != lax.rem(source, 2))
    def _():
        copy(cols, cols, 18, sibling).wait_recv()


def spread_panels(column):
    return pl.pallas_call(
        spread_kernel,
        out_shape=(
            jax.ShapeDtypeStruct((4, 4, 2, 3, TILE, TILE), BF16),
            jax.ShapeDtypeStruct((8, 4, TILE, TILE), BF16),
        ),
        in_specs=[spec(pltpu.VMEM)],
        out_specs=(spec(pltpu.VMEM), spec(pltpu.VMEM)),
        scratch_shapes=[
            pltpu.SemaphoreType.DMA((19,)),
            pltpu.SemaphoreType.DMA((19,)),
            pltpu.SemaphoreType.DMA,
        ],
        compiler_params=pltpu.CompilerParams(
            collective_id=2, has_side_effects=True, vmem_limit_bytes=VMEM_LIMIT
        ),
        cost_estimate=pl.CostEstimate(flops=0, bytes_accessed=2**23, transcendentals=0),
        name="spread",
    )(column)


def finish_kernel(
    targets,
    where,
    front,
    arrived,
    rows,
    cols,
    lower,
    inverse,
    out,
    factor_cols,
    row_from,
    col_from,
    seen,
):
    l = pl.program_id(0)
    p = where[0]
    q = where[1]

    @pl.when(l == 0)
    def _():
        index_rows(targets, p, row_from, seen)
        index_cols(targets, q, col_from)
        for m in range(8):
            wide = jnp.concatenate([cols[m, f] for f in range(4)], axis=1)
            solved = lax.dot_general(wide, inverse[...], NT, preferred_element_type=F32)
            factor_cols[m * TILE : (m + 1) * TILE, :] = solved.astype(BF16)

        @pl.when(q < 4)
        def _():
            factor_cols[:TILE, :] = jnp.zeros((TILE, 4 * TILE), BF16)

    natural = l * ROWS + p
    wide = jnp.concatenate([rows[f, 0, 0, 0] for f in range(4)], axis=1)
    solved = lax.dot_general(wide, inverse[...], NT, preferred_element_type=F32)
    pivot = jnp.concatenate([lower[jnp.minimum(natural, 3) * 4 + f] for f in range(4)], axis=1)
    solved = jnp.where(natural < 4, pivot, solved)
    panel_of = lax.broadcasted_iota(jnp.int32, (TILE, 4 * TILE), 1) // 256
    live = jnp.where(panel_of < natural // 2, solved, 0.0)
    product = lax.dot_general(
        live.astype(BF16), factor_cols[...], NT, preferred_element_type=F32
    )
    out[...] = front[...].astype(F32) - product
    for c in range(2):
        row = row_from[c * 24 + l]
        for m in range(8):
            col = col_from[c * 8 + m]

            @pl.when((row >= 0) & (col >= 0))
            def _(row=row, col=col, m=m):
                out[:, m * TILE : (m + 1) * TILE] += arrived[row + col].astype(F32)

    for f in range(4):

        @pl.when(q == f)
        def _(f=f):
            out[:, :TILE] = solved[:, f * TILE : (f + 1) * TILE]


def finish(targets, where, front, arrived, rows, cols, lower, inverse):
    return pl.pallas_call(
        finish_kernel,
        out_shape=jax.ShapeDtypeStruct((24 * TILE, 8 * TILE), F32),
        grid=(24,),
        in_specs=[
            spec(pltpu.SMEM),
            spec(pltpu.SMEM),
            pl.BlockSpec((TILE, 8 * TILE), lambda l: (l, 0)),
            spec(pltpu.VMEM),
            pl.BlockSpec(
                (4, 1, 1, 1, TILE, TILE), lambda l: (0, l // 6, l % 6 // 3, l % 3, 0, 0)
            ),
            spec(pltpu.VMEM),
            spec(pltpu.VMEM),
            spec(pltpu.VMEM),
        ],
        out_specs=pl.BlockSpec((TILE, 8 * TILE), lambda l: (l, 0)),
        scratch_shapes=[
            pltpu.VMEM((8 * TILE, 4 * TILE), BF16),
            pltpu.SMEM((48,), jnp.int32),
            pltpu.SMEM((16,), jnp.int32),
            pltpu.SMEM((ROWS,), jnp.int32),
        ],
        compiler_params=pltpu.CompilerParams(vmem_limit_bytes=VMEM_LIMIT),
        cost_estimate=pl.CostEstimate(flops=2**33, bytes_accessed=32 * 2**20, transcendentals=0),
        name="finish",
    )(targets, where, front, arrived, rows, cols, lower, inverse)


def shards(front_block, child_blocks, row_offsets, tile_targets):
    where = jnp.stack([lax.axis_index("row"), lax.axis_index("col")]).astype(jnp.int32)
    offsets = row_offsets.reshape(2, 128, TILE)
    picked, corner_part = place(
        tile_targets, where, offsets, child_blocks, front_block[:TILE, :TILE]
    )
    arrived = lax.all_to_all(
        picked.reshape(DEVICES, 2, TILE, TILE), ("row", "col"), 0, 0, tiled=True
    ).reshape(DEVICES * 2, TILE, TILE)
    corner = sum_corner(corner_part.reshape(DEVICES, 16, TILE))
    lower, inverse = factor(corner.reshape(16, TILE, TILE))
    column = first_column(tile_targets, where, front_block, arrived)
    rows, cols = spread_panels(column.reshape(4, 2, 3, TILE, TILE))
    return finish(tile_targets, where, front_block, arrived, rows, cols, lower, inverse)


def solution(mesh):
    return jax.shard_map(
        shards,
        mesh=mesh,
        in_specs=(P("row", "col"), P(None, "row", "col"), P(), P()),
        out_specs=P("row", "col"),
        check_vma=False,
    )
```

```python
import jax
import jax.numpy as jnp
from jax import lax
from jax.experimental import pallas as pl
from jax.experimental.pallas import tpu as pltpu
from jax.sharding import PartitionSpec as P

TILE = 128
ROWS = 8
COLS = 16
DEVICES = ROWS * COLS
MESH = pl.DeviceIdType.MESH
VMEM_LIMIT = 56 * 2**20
BF16 = jnp.bfloat16
F32 = jnp.float32
NT = (((1,), (1,)), ((), ()))


def spec(space):
    return pl.BlockSpec(memory_space=space)


def iota(dim):
    return lax.broadcasted_iota(jnp.int32, (TILE, TILE), dim)


def one_hot(offsets):
    return jnp.where(iota(0) == offsets, 1.0, 0.0).astype(BF16)


def place_kernel(targets, where, offsets, child, picked, shifted, tiles, rank, seen, sent):
    c = pl.program_id(0)
    p = where[0]
    q = where[1]

    for d in range(ROWS):
        seen[d] = 0

    def order(l, carry):
        owner = lax.rem(targets[c, l * ROWS + p], ROWS)
        rank[l] = owner * COLS * 2 + seen[owner]
        seen[owner] = seen[owner] + 1
        return carry

    lax.fori_loop(0, 16, order, 0)

    def tile_offsets(t):
        both = offsets[:, pl.ds(pl.multiple_of(t * TILE, TILE), TILE)]
        return jnp.where(c == 0, both[:1], both[1:])

    for l in range(16):
        hot = one_hot(tile_offsets(l * ROWS + p))
        moved = jnp.dot(
            hot, child[0, l * TILE : (l + 1) * TILE, :], preferred_element_type=F32
        )
        shifted[l * TILE : (l + 1) * TILE, :] = moved.astype(BF16)
    for k in range(4):
        hot = one_hot(tile_offsets(k * COLS + q)).T
        front_col = targets[c, k * COLS + q]
        base = lax.rem(front_col, COLS) * 2
        for part in range(4):
            rows = shifted[part * 512 : (part + 1) * 512, k * TILE : (k + 1) * TILE]
            placed = jnp.dot(rows, hot, preferred_element_type=F32)
            for s in range(4):
                l = part * 4 + s
                tile = placed[s * TILE : (s + 1) * TILE]
                held = tiles.at[(c * 4 + k) * 16 + l]
                held[...] = tile.astype(BF16)
                pltpu.make_async_copy(held, picked.at[rank[l] + base], sent).start()

    @pl.when(c == 1)
    def _():
        pltpu.make_async_copy(tiles, tiles, sent).wait()


def place(targets, where, offsets, child):
    return pl.pallas_call(
        place_kernel,
        out_shape=jax.ShapeDtypeStruct((DEVICES * 2, TILE, TILE), BF16),
        grid=(2,),
        in_specs=[
            spec(pltpu.SMEM),
            spec(pltpu.SMEM),
            spec(pltpu.VMEM),
            pl.BlockSpec((1, 16 * TILE, 4 * TILE), lambda c: (c, 0, 0)),
        ],
        out_specs=spec(pl.ANY),
        scratch_shapes=[
            pltpu.VMEM((16 * TILE, 4 * TILE), BF16),
            pltpu.VMEM((DEVICES, TILE, TILE), BF16),
            pltpu.SMEM((16,), jnp.int32),
            pltpu.SMEM((ROWS,), jnp.int32),
            pltpu.SemaphoreType.DMA,
        ],
        compiler_params=pltpu.CompilerParams(vmem_limit_bytes=VMEM_LIMIT),
        cost_estimate=pl.CostEstimate(flops=2**31, bytes_accessed=14 * 2**20, transcendentals=0),
        name="place",
    )(targets, where, offsets, child)


def mm(a, b):
    return jnp.dot(a, b, precision=lax.Precision.HIGHEST, preferred_element_type=F32)


def mm_nt(a, b):
    return lax.dot_general(
        a, b, NT, precision=lax.Precision.HIGHEST, preferred_element_type=F32
    )


def factor_tile(a):
    blocks = TILE // 8
    sub = lax.broadcasted_iota(jnp.int32, (8, 1), 0)
    eye = jnp.where(iota(0) == iota(1), 1.0, 0.0)
    upper = [a[i * 8 : (i + 1) * 8] for i in range(blocks)]
    inverse = [eye[i * 8 : (i + 1) * 8] for i in range(blocks)]
    for s in range(0, TILE, 2):
        b, r = s // 8, s % 8
        u1, u2 = upper[b][r : r + 1], upper[b][r + 1 : r + 2]
        v1, v2 = inverse[b][r : r + 1], inverse[b][r + 1 : r + 2]
        a11, a12, a22 = u1[:, s : s + 1], u1[:, s + 1 : s + 2], u2[:, s + 1 : s + 2]
        scale = 1.0 / a11
        scale2 = a11 / (a11 * a22 - a12 * a12)
        ratio = a12 * scale
        w1, x1 = u1 * scale, v1 * scale
        w2, x2 = (u2 - ratio * u1) * scale2, (v2 - ratio * v1) * scale2
        w3, x3 = w1 - ratio * w2, x1 - ratio * x2
        for i in range(b, blocks):
            c1, c2 = upper[i][:, s : s + 1], upper[i][:, s + 1 : s + 2]
            if i == b:
                second = jnp.where(sub == r + 1, c1, 0.0)
                upper[i] = upper[i] - second * w1
                inverse[i] = inverse[i] - second * x1
                if r == 6:
                    continue
                c1 = jnp.where(sub > r + 1, c1, 0.0)
                c2 = jnp.where(sub > r + 1, c2, 0.0)
            upper[i] = upper[i] - c1 * w3 - c2 * w2
            inverse[i] = inverse[i] - c1 * x3 - c2 * x2
    u = jnp.concatenate(upper, axis=0)
    inv = jnp.concatenate(inverse, axis=0)
    diagonal = jnp.sum(jnp.where(iota(0) == iota(1), u, 0.0), axis=1, keepdims=True)
    root = lax.rsqrt(diagonal)
    u = jnp.where(iota(1) >= iota(0), u * root, 0.0)
    return u.T, inv * root


def factor_corner(corner, lower, inverse, work, inv, between, after):
    def tile(i, j):
        return corner[j, i].astype(F32)

    for i in range(4):
        for j in range(i + 1):
            one = tile(i, j)
            work[i * 4 + j] = (one + tile(j, i).T) * 0.5 if i // 2 == j // 2 else one
    lower[...] = jnp.zeros_like(lower)

    def panel(j, carry):
        between(j)
        pivot, pivot_inv = factor_tile(work[j * 5])
        lower[j * 5] = pivot
        inv[j * 5] = pivot_inv

        def solve(i, carry):
            lower[i * 4 + j] = mm_nt(work[i * 4 + j], pivot_inv)
            return carry

        lax.fori_loop(j + 1, 4, solve, 0)

        def update_row(i, carry):
            def update(k, carry):
                work[i * 4 + k] -= mm_nt(lower[i * 4 + j], lower[k * 4 + j])
                return carry

            return lax.fori_loop(j + 1, i + 1, update, carry)

        lax.fori_loop(j + 1, 4, update_row, 0)
        return carry

    lax.fori_loop(0, 4, panel, 0)
    after()
    inverse[...] = jnp.zeros_like(inverse)
    for j in range(4):
        column = {j: inv[j * 5]}
        for i in range(j + 1, 4):
            total = mm(lower[i * 4 + j], column[j])
            for k in range(j + 1, i):
                total = total + mm(lower[i * 4 + k], column[k])
            column[i] = -mm(inv[i * 5], total)
        for i in range(j, 4):
            block = column[i].T.astype(BF16)
            inverse[j * TILE : (j + 1) * TILE, i * TILE : (i + 1) * TILE] = block


def index_rows(targets, p, row_from, seen):
    def clear(i, carry):
        row_from[i] = -1
        return carry

    lax.fori_loop(0, 48, clear, 0)
    for c in range(2):
        for d in range(ROWS):
            seen[d] = 0

        def visit(t, carry):
            goal = targets[c, t]

            @pl.when(lax.rem(goal, ROWS) == p)
            def _():
                source = lax.rem(t, ROWS)
                row_from[c * 24 + goal // ROWS] = source * COLS * 2 + seen[source]
                seen[source] = seen[source] + 1

            return carry

        lax.fori_loop(0, 128, visit, 0)


def index_cols(targets, q, col_from):
    for i in range(16):
        col_from[i] = -1
    for c in range(2):

        def visit(t, carry):
            goal = targets[c, t]

            @pl.when(lax.rem(goal, COLS) == q)
            def _():
                col_from[c * 8 + goal // COLS] = lax.rem(t, COLS) * 2

            return carry

        lax.fori_loop(0, 64, visit, 0)


def column_kernel(
    targets, where, front, arrived, column, held, row_from, col_from, seen, landed
):
    p = where[0]
    q = where[1]

    @pl.when(q < 4)
    def _():
        index_rows(targets, p, row_from, seen)
        index_cols(targets, q, col_from)

        def fetch(i, carry):
            row, col = row_from[i], col_from[i // 24 * 8]

            @pl.when((row >= 0) & (col >= 0))
            def _():
                pltpu.make_async_copy(
                    arrived.at[jnp.maximum(row + col, 0)], held.at[i], landed.at[i]
                ).start()

            return carry

        lax.fori_loop(0, 48, fetch, 0)

        def tile(l, carry):
            total = front[pl.ds(pl.multiple_of(l * TILE, TILE), TILE), :].astype(F32)
            for c in range(2):
                row, col = row_from[c * 24 + l], col_from[c * 8]
                here = (row >= 0) & (col >= 0)

                @pl.when(here)
                def _(c=c):
                    i = c * 24 + l
                    pltpu.make_async_copy(held.at[i], held.at[i], landed.at[i]).wait()

                total = total + jnp.where(here, held[c * 24 + l].astype(F32), 0.0)
            column[l] = total.astype(BF16)
            return carry

        lax.fori_loop(0, 24, tile, 0)


def first_column(targets, where, front, arrived):
    return pl.pallas_call(
        column_kernel,
        out_shape=jax.ShapeDtypeStruct((24, TILE, TILE), BF16),
        grid=(1,),
        in_specs=[
            spec(pltpu.SMEM),
            spec(pltpu.SMEM),
            pl.BlockSpec((24 * TILE, TILE), lambda i: (0, 0)),
            spec(pl.ANY),
        ],
        out_specs=pl.BlockSpec((24, TILE, TILE), lambda i: (0, 0, 0)),
        scratch_shapes=[
            pltpu.VMEM((48, TILE, TILE), BF16),
            pltpu.SMEM((48,), jnp.int32),
            pltpu.SMEM((16,), jnp.int32),
            pltpu.SMEM((ROWS,), jnp.int32),
            pltpu.SemaphoreType.DMA((48,)),
        ],
        compiler_params=pltpu.CompilerParams(vmem_limit_bytes=VMEM_LIMIT),
        cost_estimate=pl.CostEstimate(flops=2**20, bytes_accessed=2**22, transcendentals=0),
        name="column",
    )(targets, where, front, arrived)


def spread_kernel(
    column, rows, cols, lower, inverse, corner, work, inv, sends, recvs, corner_sends, corner_recvs, local
):
    p = lax.axis_index("row")
    q = lax.axis_index("col")
    z, core = p // 2, lax.rem(p, 2)
    x, y = q // 4, lax.rem(q, 4)

    def at_x(d):
        return (p, lax.rem(x + d, 4) * 4 + y)

    def at_y(d):
        return (p, x * 4 + lax.rem(y + d, 4))

    def at_z(d):
        return (lax.rem(z + d, 4) * 2 + core, q)

    def at_row(d):
        return (lax.rem(p + d, ROWS), q)

    barrier = pltpu.get_barrier_semaphore()
    for d in (1, 2, 3):
        for peer in (at_x(d), at_y(d)):
            pl.semaphore_signal(barrier, inc=1, device_id=peer, device_id_type=MESH)
    for d in range(1, ROWS):
        pl.semaphore_signal(barrier, inc=1, device_id=at_row(d), device_id_type=MESH)
    pl.semaphore_wait(barrier, 13)

    def copy(src, dst, slot, peer):
        return pltpu.make_async_remote_copy(
            src, dst, sends.at[slot], recvs.at[slot], device_id=peer, device_id_type=MESH
        )

    def corner_copy(src, dst, sent, landed, peer):
        return pltpu.make_async_remote_copy(
            src,
            dst,
            corner_sends.at[sent],
            corner_recvs.at[landed],
            device_id=peer,
            device_id_type=MESH,
        )

    for r in range(4):

        @pl.when((q < 4) & (p == r))
        def _(r=r):
            first = column.at[0, 0, 0]
            for d in range(1, ROWS):
                corner_copy(first, corner.at[y, r], d - 1, r, at_row(d)).start()
            own = pltpu.make_async_copy(first, corner.at[y, r], local)
            own.start()
            own.wait()

    @pl.when(x == 0)
    def _():
        for d in (1, 2, 3):
            copy(column.at[d], rows.at[y, d], d - 1, at_x(d)).start()
        own = pltpu.make_async_copy(column.at[0], rows.at[y, 0], local)
        own.start()
        own.wait()

    for r in range(4):

        @pl.when((q < 4) & (p != r))
        def _(r=r):
            corner_copy(corner.at[y, r], corner.at[y, r], 0, r, at_row(1)).wait_recv()

    @pl.when(x == 0)
    def _():
        for d in (1, 2, 3):
            corner_copy(corner.at[y], corner.at[y], 6 + d, 3 + d, at_x(d)).start()

    for d in (1, 2, 3):

        @pl.when(x == d)
        def _(d=d):
            corner_copy(corner.at[y], corner.at[y], 6 + d, 3 + d, at_x(4 - d)).wait_recv()

    last = [corner_copy(corner.at[y], corner.at[y], 9 + d, 6 + d, at_y(d)) for d in (1, 2, 3)]
    for one in last:
        one.start()

    for d in (1, 2, 3):

        @pl.when(x == d)
        def _(d=d):
            copy(column.at[d], rows.at[y, d], d - 1, at_x(4 - d)).wait_recv()

    first = []
    for d in (1, 2, 3):
        half = rows.at[y, x, 0]
        first.append(copy(half, half, 2 + d, at_x(d)))
        half = rows.at[y, x, 1]
        first.append(copy(half, half, 5 + d, at_y(d)))
    for one in first:
        one.start()
    for one in first:
        one.wait_recv()
    second = []
    for d in (1, 2, 3):
        half = rows.at[y, :, 0]
        second.append(copy(half, half, 8 + d, at_y(d)))
        half = rows.at[:, x, 1]
        second.append(copy(half, half, 11 + d, at_x(d)))
    for one in second:
        one.start()
    for one in last:
        one.wait_recv()

    source = lax.rem(q, ROWS)
    lead = source // 2
    sibling = (z * 2 + 1 - core, q)

    def between(j):
        @pl.when(j == 2)
        def _():
            for one in second:
                one.wait_recv()

        @pl.when((j == 2) & (p == source))
        def _():
            for m in range(8):
                l = 2 * m + q // ROWS
                tile = rows.at[:, l // 6, lax.rem(l, 6) // 3, lax.rem(l, 3)]
                own = pltpu.make_async_copy(tile, cols.at[m], local)
                own.start()
                own.wait()
            for d in (1, 2, 3):
                copy(cols, cols, 14 + d, at_z(d)).start()
            copy(cols, cols, 18, sibling).start()

    def after():
        for d in (1, 2, 3):

            @pl.when((core == lax.rem(source, 2)) & (lax.rem(lead + d, 4) == z))
            def _(d=d):
                copy(cols, cols, 14 + d, at_z(4 - d)).wait_recv()
                copy(cols, cols, 18, sibling).start()

    factor_corner(corner, lower, inverse, work, inv, between, after)

    @pl.when(core != lax.rem(source, 2))
    def _():
        copy(cols, cols, 18, sibling).wait_recv()

    @pl.when(core == lax.rem(source, 2))
    def _():
        copy(cols, cols, 18, sibling).wait_send()

    @pl.when(p == source)
    def _():
        for d in (1, 2, 3):
            copy(cols, cols, 14 + d, at_z(d)).wait_send()

    for one in last + first + second:
        one.wait_send()

    @pl.when(x == 0)
    def _():
        for d in (1, 2, 3):
            copy(column.at[d], rows.at[y, d], d - 1, at_x(d)).wait_send()
            corner_copy(corner.at[y], corner.at[y], 6 + d, 3 + d, at_x(d)).wait_send()

    @pl.when((q < 4) & (p < 4))
    def _():
        for d in range(1, ROWS):
            first = column.at[0, 0, 0]
            corner_copy(first, first, d - 1, 0, at_row(d)).wait_send()


def spread_panels(column):
    return pl.pallas_call(
        spread_kernel,
        out_shape=(
            jax.ShapeDtypeStruct((4, 4, 2, 3, TILE, TILE), BF16),
            jax.ShapeDtypeStruct((8, 4, TILE, TILE), BF16),
            jax.ShapeDtypeStruct((16, TILE, TILE), F32),
            jax.ShapeDtypeStruct((4 * TILE, 4 * TILE), BF16),
        ),
        in_specs=[spec(pltpu.VMEM)],
        out_specs=(spec(pltpu.VMEM),) * 4,
        scratch_shapes=[
            pltpu.VMEM((4, 4, TILE, TILE), BF16),
            pltpu.VMEM((16, TILE, TILE), F32),
            pltpu.VMEM((16, TILE, TILE), F32),
            pltpu.SemaphoreType.DMA((19,)),
            pltpu.SemaphoreType.DMA((19,)),
            pltpu.SemaphoreType.DMA((13,)),
            pltpu.SemaphoreType.DMA((10,)),
            pltpu.SemaphoreType.DMA,
        ],
        compiler_params=pltpu.CompilerParams(
            collective_id=2, has_side_effects=True, vmem_limit_bytes=VMEM_LIMIT
        ),
        cost_estimate=pl.CostEstimate(flops=2**30, bytes_accessed=2**23, transcendentals=0),
        name="spread",
    )(column)


def finish_kernel(
    targets,
    where,
    front,
    arrived,
    rows,
    cols,
    lower,
    inverse,
    out,
    factor_cols,
    solved,
    live,
    row_from,
    col_from,
    seen,
):
    g = pl.program_id(0)
    p = where[0]
    q = where[1]

    @pl.when(g == 0)
    def _():
        index_rows(targets, p, row_from, seen)
        index_cols(targets, q, col_from)
        for m in range(8):
            wide = jnp.concatenate([cols[m, f] for f in range(4)], axis=1)
            found = jnp.dot(wide, inverse[...], preferred_element_type=F32)
            factor_cols[:, m * TILE : (m + 1) * TILE] = found.astype(BF16).T

    wide = jnp.concatenate(
        [rows[f, 0, 0].reshape(3 * TILE, TILE) for f in range(4)], axis=1
    )
    found = jnp.dot(wide, inverse[...], preferred_element_type=F32)
    solved[...] = found
    live[...] = found.astype(BF16)

    @pl.when((g == 0) & (p < 4))
    def _():
        for f in range(4):
            tile = lower[p * 4 + f]
            at = slice(f * TILE, (f + 1) * TILE)
            solved[:TILE, at] = tile
            live[:TILE, at] = jnp.where(f // 2 < p // 2, tile, 0.0).astype(BF16)

    for pair in range(4):
        at = slice(pair * 256, (pair + 1) * 256)
        product = jnp.dot(live[...], factor_cols[:, at], preferred_element_type=F32)
        for t in range(3):
            for m in (pair * 2, pair * 2 + 1):
                down = slice(t * TILE, (t + 1) * TILE)
                across = slice(m * TILE, (m + 1) * TILE)
                total = front[down, across].astype(F32)
                total = total - product[down, (m % 2) * TILE : (m % 2 + 1) * TILE]
                for c in range(2):
                    row = row_from[c * 24 + g * 3 + t]
                    col = col_from[c * 8 + m]
                    tile = arrived[jnp.maximum(row, 0) + jnp.maximum(col, 0)]
                    here = (row >= 0) & (col >= 0)
                    total = total + jnp.where(here, tile.astype(F32), 0.0)
                out[down, across] = total

    for f in range(4):

        @pl.when(q == f)
        def _(f=f):
            out[:, :TILE] = solved[:, f * TILE : (f + 1) * TILE]


def finish(targets, where, front, arrived, rows, cols, lower, inverse):
    return pl.pallas_call(
        finish_kernel,
        out_shape=jax.ShapeDtypeStruct((24 * TILE, 8 * TILE), F32),
        grid=(8,),
        in_specs=[
            spec(pltpu.SMEM),
            spec(pltpu.SMEM),
            pl.BlockSpec((3 * TILE, 8 * TILE), lambda g: (g, 0)),
            spec(pltpu.VMEM),
            pl.BlockSpec((4, 1, 1, 3, TILE, TILE), lambda g: (0, g // 2, g % 2, 0, 0, 0)),
            spec(pltpu.VMEM),
            spec(pltpu.VMEM),
            spec(pltpu.VMEM),
        ],
        out_specs=pl.BlockSpec((3 * TILE, 8 * TILE), lambda g: (g, 0)),
        scratch_shapes=[
            pltpu.VMEM((4 * TILE, 8 * TILE), BF16),
            pltpu.VMEM((3 * TILE, 4 * TILE), F32),
            pltpu.VMEM((3 * TILE, 4 * TILE), BF16),
            pltpu.SMEM((48,), jnp.int32),
            pltpu.SMEM((16,), jnp.int32),
            pltpu.SMEM((ROWS,), jnp.int32),
        ],
        compiler_params=pltpu.CompilerParams(vmem_limit_bytes=VMEM_LIMIT),
        cost_estimate=pl.CostEstimate(flops=2**33, bytes_accessed=32 * 2**20, transcendentals=0),
        name="finish",
    )(targets, where, front, arrived, rows, cols, lower, inverse)


def shards(front_block, child_blocks, row_offsets, tile_targets):
    where = jnp.stack([lax.axis_index("row"), lax.axis_index("col")]).astype(jnp.int32)
    picked = place(tile_targets, where, row_offsets, child_blocks)
    arrived = lax.all_to_all(
        picked.reshape(DEVICES, 2, TILE, TILE), ("row", "col"), 0, 0, tiled=True
    ).reshape(DEVICES * 2, TILE, TILE)
    column = first_column(tile_targets, where, front_block, arrived)
    rows, cols, lower, inverse = spread_panels(column.reshape(4, 2, 3, TILE, TILE))
    return finish(tile_targets, where, front_block, arrived, rows, cols, lower, inverse)


def solution(mesh):
    return jax.shard_map(
        shards,
        mesh=mesh,
        in_specs=(P("row", "col"), P(None, "row", "col"), P(), P()),
        out_specs=P("row", "col"),
        check_vma=False,
    )
```

```python
import jax
import jax.numpy as jnp
from jax import lax
from jax.experimental import pallas as pl
from jax.experimental.pallas import tpu as pltpu
from jax.sharding import PartitionSpec as P

TILE = 128
ROWS = 8
COLS = 16
DEVICES = ROWS * COLS
MESH = pl.DeviceIdType.MESH
BF16 = jnp.bfloat16
F32 = jnp.float32
NT = (((1,), (1,)), ((), ()))


def spec(space):
    return pl.BlockSpec(memory_space=space)


def iota(dim):
    return lax.broadcasted_iota(jnp.int32, (TILE, TILE), dim)


def one_hot(offsets):
    return jnp.where(iota(0) == offsets, 1.0, 0.0).astype(BF16)


def place_kernel(targets, where, offsets, child, picked, shifted, tiles, rank, seen, sent):
    c = pl.program_id(0)
    p = where[0]
    q = where[1]

    for d in range(ROWS):
        seen[d] = 0

    def order(l, carry):
        owner = lax.rem(targets[c, l * ROWS + p], ROWS)
        rank[l] = owner * COLS * 2 + seen[owner]
        seen[owner] = seen[owner] + 1
        return carry

    lax.fori_loop(0, 16, order, 0)

    def tile_offsets(t):
        both = offsets[:, pl.ds(pl.multiple_of(t * TILE, TILE), TILE)]
        return jnp.where(c == 0, both[:1], both[1:])

    for l in range(16):
        hot = one_hot(tile_offsets(l * ROWS + p))
        moved = jnp.dot(
            hot, child[0, l * TILE : (l + 1) * TILE, :], preferred_element_type=F32
        )
        shifted[l * TILE : (l + 1) * TILE, :] = moved.astype(BF16)
    for k in range(4):
        hot = one_hot(tile_offsets(k * COLS + q)).T
        front_col = targets[c, k * COLS + q]
        base = lax.rem(front_col, COLS) * 2
        for part in range(4):
            rows = shifted[part * 512 : (part + 1) * 512, k * TILE : (k + 1) * TILE]
            placed = jnp.dot(rows, hot, preferred_element_type=F32)
            for s in range(4):
                l = part * 4 + s
                tile = placed[s * TILE : (s + 1) * TILE]
                held = tiles.at[(c * 4 + k) * 16 + l]
                held[...] = tile.astype(BF16)
                pltpu.make_async_copy(held, picked.at[rank[l] + base], sent).start()

    @pl.when(c == 1)
    def _():
        pltpu.make_async_copy(tiles, tiles, sent).wait()


def place(targets, where, offsets, child):
    return pl.pallas_call(
        place_kernel,
        out_shape=jax.ShapeDtypeStruct((DEVICES * 2, TILE, TILE), BF16),
        grid=(2,),
        in_specs=[
            spec(pltpu.SMEM),
            spec(pltpu.SMEM),
            spec(pltpu.VMEM),
            pl.BlockSpec((1, 16 * TILE, 4 * TILE), lambda c: (c, 0, 0)),
        ],
        out_specs=spec(pl.ANY),
        scratch_shapes=[
            pltpu.VMEM((16 * TILE, 4 * TILE), BF16),
            pltpu.VMEM((DEVICES, TILE, TILE), BF16),
            pltpu.SMEM((16,), jnp.int32),
            pltpu.SMEM((ROWS,), jnp.int32),
            pltpu.SemaphoreType.DMA,
        ],
        compiler_params=pltpu.CompilerParams(vmem_limit_bytes=56 * 2**20),
        cost_estimate=pl.CostEstimate(flops=2**31, bytes_accessed=14 * 2**20, transcendentals=0),
        name="place",
    )(targets, where, offsets, child)


def mm(a, b):
    return jnp.dot(a, b, precision=lax.Precision.HIGHEST, preferred_element_type=F32)


def mm_nt(a, b):
    return lax.dot_general(
        a, b, NT, precision=lax.Precision.HIGHEST, preferred_element_type=F32
    )


def reciprocal(x):
    r = pl.reciprocal(x, approx=True)
    r = r * (2.0 - x * r)
    return r * (2.0 - x * r)


def lane(x, s):
    return jnp.take_along_axis(x, jnp.full((8, TILE), s, jnp.int32), axis=1)


def every(x, r):
    return jnp.broadcast_to(x[r : r + 1], (8, TILE))


def factor_tile(a):
    blocks = TILE // 8
    sub = lax.broadcasted_iota(jnp.int32, (8, TILE), 0)
    eye = jnp.where(iota(0) == iota(1), 1.0, 0.0)
    upper = [a[i * 8 : (i + 1) * 8] for i in range(blocks)]
    inverse = [eye[i * 8 : (i + 1) * 8] for i in range(blocks)]
    for s in range(0, TILE, 4):
        b, r = s // 8, s % 8
        c = [lane(upper[b], s + k) for k in range(4)]
        a00, a01, a02, a03 = (every(c[k], r) for k in range(4))
        a11, a12, a13 = (every(c[k], r + 1) for k in range(1, 4))
        a22, a23 = (every(c[k], r + 2) for k in range(2, 4))
        a33 = every(c[3], r + 3)
        det = reciprocal(a00 * a11 - a01 * a01)
        p00, p01, p11 = a11 * det, -a01 * det, a00 * det
        t20, t21 = a02 * p00 + a12 * p01, a02 * p01 + a12 * p11
        t30, t31 = a03 * p00 + a13 * p01, a03 * p01 + a13 * p11
        r22 = a22 - t20 * a02 - t21 * a12
        r23 = a23 - t20 * a03 - t21 * a13
        r33 = a33 - t30 * a03 - t31 * a13
        det = reciprocal(r22 * r33 - r23 * r23)
        i22, i23, i33 = r33 * det, -r23 * det, r22 * det
        ratio1 = a01 * reciprocal(a00)
        ratio3 = r23 * reciprocal(r22)
        for strips in (upper, inverse):
            u = [every(strips[b], r + k) for k in range(4)]
            l2 = u[2] - t20 * u[0] - t21 * u[1]
            l3 = u[3] - t30 * u[0] - t31 * u[1]
            w2 = i22 * l2 + i23 * l3
            w3 = i23 * l2 + i33 * l3
            w0 = p00 * u[0] + p01 * u[1] - t20 * w2 - t30 * w3
            w1 = p01 * u[0] + p11 * u[1] - t21 * w2 - t31 * w3
            one = strips[b]
            one = jnp.where(sub == r + 1, u[1] - ratio1 * u[0], one)
            one = jnp.where(sub == r + 2, l2, one)
            one = jnp.where(sub == r + 3, l3 - ratio3 * l2, one)
            if r == 0:
                after = strips[b] - c[0] * w0 - c[1] * w1 - c[2] * w2 - c[3] * w3
                one = jnp.where(sub > 3, after, one)
            if strips is upper:
                rows = [[lane(upper[i], s + k) for k in range(4)] for i in range(b + 1, blocks)]
            strips[b] = one
            for i in range(b + 1, blocks):
                e = rows[i - b - 1]
                strips[i] = strips[i] - e[0] * w0 - e[1] * w1 - e[2] * w2 - e[3] * w3
    u = jnp.concatenate(upper, axis=0)
    inv = jnp.concatenate(inverse, axis=0)
    diagonal = jnp.sum(jnp.where(iota(0) == iota(1), u, 0.0), axis=1, keepdims=True)
    root = lax.rsqrt(diagonal)
    u = jnp.where(iota(1) >= iota(0), u * root, 0.0)
    return u.T, inv * root


def factor_corner(corner, lower, inverse, work, inv, between, after):
    def tile(i, j):
        return corner[j, i].astype(F32)

    for i in range(4):
        for j in range(i + 1):
            one = tile(i, j)
            work[i * 4 + j] = (one + tile(j, i).T) * 0.5 if i // 2 == j // 2 else one
    lower[...] = jnp.zeros_like(lower)

    def panel(j, carry):
        between(j)
        pivot, pivot_inv = factor_tile(work[j * 5])
        lower[j * 5] = pivot
        inv[j * 5] = pivot_inv

        def solve(i, carry):
            lower[i * 4 + j] = mm_nt(work[i * 4 + j], pivot_inv)
            return carry

        lax.fori_loop(j + 1, 4, solve, 0)

        def update_row(i, carry):
            def update(k, carry):
                work[i * 4 + k] -= mm_nt(lower[i * 4 + j], lower[k * 4 + j])
                return carry

            return lax.fori_loop(j + 1, i + 1, update, carry)

        lax.fori_loop(j + 1, 4, update_row, 0)
        return carry

    lax.fori_loop(0, 4, panel, 0)
    after()
    inverse[...] = jnp.zeros_like(inverse)
    for j in range(4):
        column = {j: inv[j * 5]}
        for i in range(j + 1, 4):
            total = mm(lower[i * 4 + j], column[j])
            for k in range(j + 1, i):
                total = total + mm(lower[i * 4 + k], column[k])
            column[i] = -mm(inv[i * 5], total)
        for i in range(j, 4):
            block = column[i].T.astype(BF16)
            inverse[j * TILE : (j + 1) * TILE, i * TILE : (i + 1) * TILE] = block


ABSENT = DEVICES * 2


def index_kernel(targets, where, row_from, col_from, seen):
    p = where[0]
    q = where[1]

    def clear_rows(i, carry):
        row_from[i] = ABSENT
        return carry

    def clear_cols(i, carry):
        col_from[i] = ABSENT
        return carry

    lax.fori_loop(0, 48, clear_rows, 0)
    lax.fori_loop(0, 16, clear_cols, 0)
    for c in range(2):
        for d in range(ROWS):
            seen[d] = 0

        def visit_row(t, carry):
            goal = targets[c, t]

            @pl.when(lax.rem(goal, ROWS) == p)
            def _():
                source = lax.rem(t, ROWS)
                row_from[c * 24 + goal // ROWS] = source * COLS * 2 + seen[source]
                seen[source] = seen[source] + 1

            return carry

        lax.fori_loop(0, 128, visit_row, 0)

        def visit_col(t, carry):
            goal = targets[c, t]

            @pl.when(lax.rem(goal, COLS) == q)
            def _():
                col_from[c * 8 + goal // COLS] = lax.rem(t, COLS) * 2

            return carry

        lax.fori_loop(0, 64, visit_col, 0)


def index_tiles(targets, where):
    return pl.pallas_call(
        index_kernel,
        out_shape=(
            jax.ShapeDtypeStruct((48,), jnp.int32),
            jax.ShapeDtypeStruct((16,), jnp.int32),
        ),
        in_specs=[spec(pltpu.SMEM), spec(pltpu.SMEM)],
        out_specs=(spec(pltpu.SMEM), spec(pltpu.SMEM)),
        scratch_shapes=[pltpu.SMEM((ROWS,), jnp.int32)],
        cost_estimate=pl.CostEstimate(flops=2**20, bytes_accessed=2**16, transcendentals=0),
        name="index",
    )(targets, where)


def column_kernel(row_from, col_from, where, front, arrived, column, heads, held, landed):
    @pl.when(where[1] < 4)
    def _():
        slots = []
        for c in range(2):
            for l in range(24):
                i = c * 24 + l
                slot = row_from[i] + col_from[c * 8]
                slots.append(slot)

                @pl.when(slot < ABSENT)
                def _(i=i, slot=slot):
                    pltpu.make_async_copy(arrived.at[slot], held.at[i], landed.at[i]).start()

        for l in range(24):
            total = front[l * TILE : (l + 1) * TILE, :].astype(F32)
            for i in (l, 24 + l):

                @pl.when(slots[i] < ABSENT)
                def _(i=i):
                    pltpu.make_async_copy(held.at[i], held.at[i], landed.at[i]).wait()

                total = total + jnp.where(slots[i] < ABSENT, held[i].astype(F32), 0.0)
            column[l] = total.astype(BF16)
            if l < 16:
                heads[l % 2, l // 2] = total.astype(BF16)


def first_column(row_from, col_from, where, front, arrived):
    return pl.pallas_call(
        column_kernel,
        out_shape=(
            jax.ShapeDtypeStruct((24, TILE, TILE), BF16),
            jax.ShapeDtypeStruct((2, 8, TILE, TILE), BF16),
        ),
        grid=(1,),
        in_specs=[
            spec(pltpu.SMEM),
            spec(pltpu.SMEM),
            spec(pltpu.SMEM),
            pl.BlockSpec((24 * TILE, TILE), lambda i: (0, 0)),
            spec(pl.ANY),
        ],
        out_specs=(
            pl.BlockSpec((24, TILE, TILE), lambda i: (0, 0, 0)),
            pl.BlockSpec((2, 8, TILE, TILE), lambda i: (0, 0, 0, 0)),
        ),
        scratch_shapes=[
            pltpu.VMEM((48, TILE, TILE), BF16),
            pltpu.SemaphoreType.DMA((48,)),
        ],
        compiler_params=pltpu.CompilerParams(vmem_limit_bytes=10 * 2**20),
        cost_estimate=pl.CostEstimate(flops=2**20, bytes_accessed=2**22, transcendentals=0),
        name="column",
    )(row_from, col_from, where, front, arrived)


def spread_kernel(
    column,
    heads,
    rows,
    cols,
    lower,
    inverse,
    corner,
    work,
    inv,
    sends,
    recvs,
    share_sends,
    share_recvs,
    corner_sends,
    corner_recvs,
    head_sends,
    head_recvs,
    pass_sends,
    pass_recvs,
    locals_,
):
    p = lax.axis_index("row")
    q = lax.axis_index("col")
    z, core = p // 2, lax.rem(p, 2)
    x, y = q // 4, lax.rem(q, 4)
    source = lax.rem(q, ROWS)
    hops = lax.rem(z + 4 - source // 2, 4)
    near = core == lax.rem(source, 2)
    sibling = (z * 2 + 1 - core, q)

    def at_x(d):
        return (p, lax.rem(x + d, 4) * 4 + y)

    def at_y(d):
        return (p, x * 4 + lax.rem(y + d, 4))

    def at_z(d):
        return (lax.rem(z + d, 4) * 2 + core, q)

    def at_row(d):
        return (lax.rem(p + d, ROWS), q)

    def at_col(d):
        return (p, lax.rem(q + d, COLS))

    barrier = pltpu.get_barrier_semaphore()
    for d in range(1, COLS):
        pl.semaphore_signal(barrier, inc=1, device_id=at_col(d), device_id_type=MESH)
    for d in range(1, ROWS):
        pl.semaphore_signal(barrier, inc=1, device_id=at_row(d), device_id_type=MESH)
    pl.semaphore_wait(barrier, COLS + ROWS - 2)

    def remote(src, dst, sent, landed, peer):
        return pltpu.make_async_remote_copy(
            src, dst, sent, landed, device_id=peer, device_id_type=MESH
        )

    def copy(part, slot, peer):
        return remote(part, part, sends.at[slot], recvs.at[slot], peer)

    def corner_copy(src, dst, sent, landed, peer):
        return remote(src, dst, corner_sends.at[sent], corner_recvs.at[landed], peer)

    def head_copy(h, f, peer):
        return remote(heads.at[h], cols.at[f], head_sends.at[h], head_recvs.at[f], peer)

    def share_copy(d):
        to = lax.rem(q + d, COLS)
        part = rows.at[y, to // 4, lax.rem(to, 4)]
        return remote(column.at[to], part, share_sends.at[d], share_recvs.at[y], at_col(d))

    def pass_copy(part, slot, peer):
        return remote(part, part, pass_sends.at[slot], pass_recvs.at[slot], peer)

    def own_copy(src, dst, slot):
        own = pltpu.make_async_copy(src, dst, locals_.at[slot])
        own.start()
        own.wait()

    first_tile = column.at[0, 0].at[pl.ds(0, 96)]
    second_part = column.at[0, 1].at[pl.ds(0, 32)]

    def first_copies(r, d):
        return (
            corner_copy(first_tile, corner.at[y, r, pl.ds(0, 96)], 2 * d - 2, r, at_row(d)),
            corner_copy(second_part, corner.at[y, r, pl.ds(96, 32)], 2 * d - 1, 10 + r, at_row(d)),
        )

    for r in range(4):

        @pl.when((q < 4) & (p == r))
        def _(r=r):
            for d in range(1, ROWS):
                for one in first_copies(r, d):
                    one.start()
            own_copy(first_tile, corner.at[y, r, pl.ds(0, 96)], 0)
            own_copy(second_part, corner.at[y, r, pl.ds(96, 32)], 0)

    for r in range(4):

        @pl.when((q < 4) & (p != r))
        def _(r=r):
            for one in first_copies(r, 1):
                one.wait_recv()

    @pl.when(x == 0)
    def _():
        for d in (1, 2, 3):
            corner_copy(corner.at[y], corner.at[y], 13 + d, 3 + d, at_x(d)).start()

    @pl.when((x == 0) & (q != p))
    def _():
        head_copy(0, y, (p, p)).start()

    @pl.when(x == 0)
    def _():
        head_copy(1, y, (p, p + 8)).start()

    @pl.when(x == 0)
    def _():
        for d in range(1, COLS):
            share_copy(d).start()
        own_copy(column.at[q], rows.at[y, 0, y], 1)

    @pl.when((x == 0) & (q == p))
    def _():
        own_copy(heads.at[0], cols.at[y], 2)

    for d in (1, 2, 3):

        @pl.when(x == d)
        def _(d=d):
            corner_copy(corner.at[y], corner.at[y], 13 + d, 3 + d, at_x(4 - d)).wait_recv()

    last = [corner_copy(corner.at[y], corner.at[y], 16 + d, 6 + d, at_y(d)) for d in (1, 2, 3)]
    for one in last:
        one.start()

    for f in range(4):

        @pl.when(q != f)
        def _(f=f):
            part = rows.at[f, x, y]
            remote(part, part, share_sends.at[0], share_recvs.at[f], at_col(1)).wait_recv()

    first = []
    for d in (1, 2, 3):
        first.append(copy(rows.at[:, x, y, 0], d - 1, at_x(d)))
        first.append(copy(rows.at[:, x, y, 1], d + 2, at_y(d)))
    for one in first:
        one.start()

    for f in range(4):

        @pl.when((p == source) & (q != f))
        def _(f=f):
            head_copy(0, f, (p, p)).wait_recv()

    low, high = cols.at[pl.ds(0, 2)], cols.at[pl.ds(2, 2)]

    @pl.when(p == source)
    def _():
        pass_copy(low, 0, at_z(1)).start()
        pass_copy(high, 1, at_z(3)).start()
        pass_copy(high, 2, at_z(1)).start()
        pass_copy(low, 3, at_z(3)).start()
        pass_copy(cols, 6, sibling).start()

    second = []
    for d in (1, 2, 3):
        second.append(copy(rows.at[:, :, y, 0], d + 5, at_y(d)))
        second.append(copy(rows.at[:, x, :, 1], d + 8, at_x(d)))
    for one in last:
        one.wait_recv()

    def between(j):
        @pl.when(j == 1)
        def _():
            for one in first:
                one.wait_recv()
            for one in second:
                one.start()

        @pl.when((j == 2) & near & (hops == 1))
        def _():
            pass_copy(low, 0, at_z(3)).wait_recv()
            pass_copy(low, 4, at_z(1)).start()
            pass_copy(high, 2, at_z(3)).wait_recv()
            pass_copy(cols, 6, sibling).start()

        @pl.when((j == 2) & near & (hops == 3))
        def _():
            pass_copy(high, 1, at_z(1)).wait_recv()
            pass_copy(high, 5, at_z(3)).start()
            pass_copy(low, 3, at_z(1)).wait_recv()
            pass_copy(cols, 6, sibling).start()

    def after():
        @pl.when(near & (hops == 2))
        def _():
            pass_copy(low, 4, at_z(3)).wait_recv()
            pass_copy(high, 5, at_z(1)).wait_recv()
            pass_copy(cols, 6, sibling).start()

    factor_corner(corner, lower, inverse, work, inv, between, after)

    for one in second:
        one.wait_recv()

    @pl.when(jnp.logical_not(near))
    def _():
        pass_copy(cols, 6, sibling).wait_recv()

    @pl.when(near)
    def _():
        pass_copy(cols, 6, sibling).wait_send()

    @pl.when(p == source)
    def _():
        pass_copy(low, 0, at_z(1)).wait_send()
        pass_copy(high, 1, at_z(3)).wait_send()
        pass_copy(high, 2, at_z(1)).wait_send()
        pass_copy(low, 3, at_z(3)).wait_send()

    @pl.when(near & (hops == 1))
    def _():
        pass_copy(low, 4, at_z(1)).wait_send()

    @pl.when(near & (hops == 3))
    def _():
        pass_copy(high, 5, at_z(3)).wait_send()

    for one in last + first + second:
        one.wait_send()

    @pl.when(x == 0)
    def _():
        for d in range(1, COLS):
            share_copy(d).wait_send()
        for d in (1, 2, 3):
            corner_copy(corner.at[y], corner.at[y], 13 + d, 3 + d, at_x(d)).wait_send()
        head_copy(1, y, (p, p + 8)).wait_send()

    @pl.when((x == 0) & (q != p))
    def _():
        head_copy(0, y, (p, p)).wait_send()

    @pl.when((q < 4) & (p < 4))
    def _():
        for d in range(1, ROWS):
            for one in first_copies(0, d):
                one.wait_send()


def spread_panels(column, heads):
    return pl.pallas_call(
        spread_kernel,
        out_shape=(
            jax.ShapeDtypeStruct((4, 4, 4, 2, 96, TILE), BF16),
            jax.ShapeDtypeStruct((4, 8, TILE, TILE), BF16),
            jax.ShapeDtypeStruct((16, TILE, TILE), F32),
            jax.ShapeDtypeStruct((4 * TILE, 4 * TILE), BF16),
        ),
        in_specs=[spec(pltpu.VMEM)] * 2,
        out_specs=(spec(pltpu.VMEM),) * 4,
        scratch_shapes=[
            pltpu.VMEM((4, 4, TILE, TILE), BF16),
            pltpu.VMEM((16, TILE, TILE), F32),
            pltpu.VMEM((16, TILE, TILE), F32),
            pltpu.SemaphoreType.DMA((12,)),
            pltpu.SemaphoreType.DMA((12,)),
            pltpu.SemaphoreType.DMA((COLS,)),
            pltpu.SemaphoreType.DMA((4,)),
            pltpu.SemaphoreType.DMA((20,)),
            pltpu.SemaphoreType.DMA((14,)),
            pltpu.SemaphoreType.DMA((2,)),
            pltpu.SemaphoreType.DMA((4,)),
            pltpu.SemaphoreType.DMA((7,)),
            pltpu.SemaphoreType.DMA((7,)),
            pltpu.SemaphoreType.DMA((3,)),
        ],
        compiler_params=pltpu.CompilerParams(
            collective_id=2, has_side_effects=True, vmem_limit_bytes=20 * 2**20
        ),
        cost_estimate=pl.CostEstimate(flops=2**30, bytes_accessed=2**23, transcendentals=0),
        name="spread",
    )(column, heads)


def finish_kernel(
    row_from,
    col_from,
    where,
    front,
    arrived,
    rows,
    cols,
    lower,
    inverse,
    out,
    factor_cols,
    solved,
    live,
    held,
    landed,
):
    g = pl.program_id(0)
    p = where[0]
    q = where[1]
    chunks = [pl.ds(i * 32, 32) for i in range(8)]

    @pl.when(g == 0)
    def _():
        for i, at in enumerate(chunks):
            pltpu.make_async_copy(arrived.at[at], held.at[at], landed.at[i]).start()
        held[ABSENT] = jnp.zeros((TILE, TILE), BF16)
        for m in range(8):
            wide = jnp.concatenate([cols[f, m] for f in range(4)], axis=1)
            found = jnp.dot(wide, inverse[...], preferred_element_type=F32)
            factor_cols[:, m * TILE : (m + 1) * TILE] = found.astype(BF16).T

    wide = jnp.concatenate(
        [rows[f] for f in range(4)], axis=1
    )
    found = jnp.dot(wide, inverse[...], preferred_element_type=F32)
    solved[...] = found
    live[...] = found.astype(BF16)

    @pl.when((g == 0) & (p < 4))
    def _():
        for f in range(4):
            tile = lower[p * 4 + f]
            at = slice(f * TILE, (f + 1) * TILE)
            solved[:TILE, at] = tile
            live[:TILE, at] = jnp.where(f // 2 < p // 2, tile, 0.0).astype(BF16)

    @pl.when(g == 0)
    def _():
        for i, at in enumerate(chunks):
            pltpu.make_async_copy(arrived.at[at], held.at[at], landed.at[i]).wait()

    for pair in range(4):
        at = slice(pair * 256, (pair + 1) * 256)
        product = jnp.dot(live[...], factor_cols[:, at], preferred_element_type=F32)
        for t in range(3):
            for m in (pair * 2, pair * 2 + 1):
                down = slice(t * TILE, (t + 1) * TILE)
                across = slice(m * TILE, (m + 1) * TILE)
                total = front[down, across].astype(F32)
                for c in range(2):
                    slot = row_from[c * 24 + g * 3 + t] + col_from[c * 8 + m]
                    total = total + held[jnp.minimum(slot, ABSENT)].astype(F32)
                out[down, across] = total - product[down, (m % 2) * TILE : (m % 2 + 1) * TILE]

    for f in range(4):

        @pl.when(q == f)
        def _(f=f):
            out[:, :TILE] = solved[:, f * TILE : (f + 1) * TILE]


def finish(row_from, col_from, where, front, arrived, rows, cols, lower, inverse):
    return pl.pallas_call(
        finish_kernel,
        out_shape=jax.ShapeDtypeStruct((24 * TILE, 8 * TILE), F32),
        grid=(8,),
        in_specs=[
            spec(pltpu.SMEM),
            spec(pltpu.SMEM),
            spec(pltpu.SMEM),
            pl.BlockSpec((3 * TILE, 8 * TILE), lambda g: (g, 0)),
            spec(pl.ANY),
            pl.BlockSpec((4, 3 * TILE, TILE), lambda g: (0, g, 0)),
            spec(pltpu.VMEM),
            spec(pltpu.VMEM),
            spec(pltpu.VMEM),
        ],
        out_specs=pl.BlockSpec((3 * TILE, 8 * TILE), lambda g: (g, 0)),
        scratch_shapes=[
            pltpu.VMEM((4 * TILE, 8 * TILE), BF16),
            pltpu.VMEM((3 * TILE, 4 * TILE), F32),
            pltpu.VMEM((3 * TILE, 4 * TILE), BF16),
            pltpu.VMEM((ABSENT + 1, TILE, TILE), BF16),
            pltpu.SemaphoreType.DMA((8,)),
        ],
        compiler_params=pltpu.CompilerParams(vmem_limit_bytes=28 * 2**20),
        cost_estimate=pl.CostEstimate(flops=2**33, bytes_accessed=32 * 2**20, transcendentals=0),
        name="finish",
    )(row_from, col_from, where, front, arrived, rows, cols, lower, inverse)


def shards(front_block, child_blocks, row_offsets, tile_targets):
    where = jnp.stack([lax.axis_index("row"), lax.axis_index("col")]).astype(jnp.int32)
    picked = place(tile_targets, where, row_offsets, child_blocks)
    arrived = lax.all_to_all(
        picked.reshape(DEVICES, 2, TILE, TILE), ("row", "col"), 0, 0, tiled=True
    ).reshape(DEVICES * 2, TILE, TILE)
    row_from, col_from = index_tiles(tile_targets, where)
    column, heads = first_column(row_from, col_from, where, front_block, arrived)
    rows, cols, lower, inverse = spread_panels(
        column.reshape(COLS, 2, 96, TILE), heads
    )
    rows = rows.reshape(4, 24 * TILE, TILE)
    return finish(row_from, col_from, where, front_block, arrived, rows, cols, lower, inverse)


def solution(mesh):
    return jax.shard_map(
        shards,
        mesh=mesh,
        in_specs=(P("row", "col"), P(None, "row", "col"), P(), P()),
        out_specs=P("row", "col"),
        check_vma=False,
    )
```

```python
import jax
import jax.numpy as jnp
from jax import lax
from jax.experimental import pallas as pl
from jax.experimental.pallas import tpu as pltpu
from jax.sharding import PartitionSpec as P

TILE = 128
ROWS = 8
COLS = 16
DEVICES = ROWS * COLS
MESH = pl.DeviceIdType.MESH
BF16 = jnp.bfloat16
F32 = jnp.float32
NT = (((1,), (1,)), ((), ()))


def spec(space):
    return pl.BlockSpec(memory_space=space)


def iota(dim):
    return lax.broadcasted_iota(jnp.int32, (TILE, TILE), dim)


def one_hot(offsets):
    return jnp.where(iota(0) == offsets, 1.0, 0.0).astype(BF16)


def place_kernel(targets, where, offsets, child, picked, shifted, tiles, rank, seen, sent):
    c = pl.program_id(0)
    p = where[0]
    q = where[1]

    for d in range(ROWS):
        seen[d] = 0

    def order(l, carry):
        owner = lax.rem(targets[c, l * ROWS + p], ROWS)
        rank[l] = owner * COLS * 2 + seen[owner]
        seen[owner] = seen[owner] + 1
        return carry

    lax.fori_loop(0, 16, order, 0)

    def tile_offsets(t):
        both = offsets[:, pl.ds(pl.multiple_of(t * TILE, TILE), TILE)]
        return jnp.where(c == 0, both[:1], both[1:])

    for l in range(16):
        hot = one_hot(tile_offsets(l * ROWS + p))
        moved = jnp.dot(
            hot, child[0, l * TILE : (l + 1) * TILE, :], preferred_element_type=F32
        )
        shifted[l * TILE : (l + 1) * TILE, :] = moved.astype(BF16)
    for k in range(4):
        hot = one_hot(tile_offsets(k * COLS + q)).T
        front_col = targets[c, k * COLS + q]
        base = lax.rem(front_col, COLS) * 2
        for part in range(4):
            rows = shifted[part * 512 : (part + 1) * 512, k * TILE : (k + 1) * TILE]
            placed = jnp.dot(rows, hot, preferred_element_type=F32)
            for s in range(4):
                l = part * 4 + s
                tile = placed[s * TILE : (s + 1) * TILE]
                held = tiles.at[(c * 4 + k) * 16 + l]
                held[...] = tile.astype(BF16)
                pltpu.make_async_copy(held, picked.at[rank[l] + base], sent).start()

    @pl.when(c == 1)
    def _():
        pltpu.make_async_copy(tiles, tiles, sent).wait()


def place(targets, where, offsets, child):
    return pl.pallas_call(
        place_kernel,
        out_shape=jax.ShapeDtypeStruct((DEVICES * 2, TILE, TILE), BF16),
        grid=(2,),
        in_specs=[
            spec(pltpu.SMEM),
            spec(pltpu.SMEM),
            spec(pltpu.VMEM),
            pl.BlockSpec((1, 16 * TILE, 4 * TILE), lambda c: (c, 0, 0)),
        ],
        out_specs=spec(pl.ANY),
        scratch_shapes=[
            pltpu.VMEM((16 * TILE, 4 * TILE), BF16),
            pltpu.VMEM((DEVICES, TILE, TILE), BF16),
            pltpu.SMEM((16,), jnp.int32),
            pltpu.SMEM((ROWS,), jnp.int32),
            pltpu.SemaphoreType.DMA,
        ],
        compiler_params=pltpu.CompilerParams(vmem_limit_bytes=56 * 2**20),
        cost_estimate=pl.CostEstimate(flops=2**31, bytes_accessed=14 * 2**20, transcendentals=0),
        name="place",
    )(targets, where, offsets, child)


def mm(a, b):
    return jnp.dot(a, b, precision=lax.Precision.HIGHEST, preferred_element_type=F32)


def mm_nt(a, b):
    return lax.dot_general(
        a, b, NT, precision=lax.Precision.HIGHEST, preferred_element_type=F32
    )


def reciprocal(x):
    r = pl.reciprocal(x, approx=True)
    r = r * (2.0 - x * r)
    return r * (2.0 - x * r)


def lane(x, s):
    return jnp.take_along_axis(x, jnp.full((8, TILE), s, jnp.int32), axis=1)


def every(x, r):
    return jnp.broadcast_to(x[r : r + 1], (8, TILE))


def factor_tile(a):
    blocks = TILE // 8
    sub = lax.broadcasted_iota(jnp.int32, (8, TILE), 0)
    eye = jnp.where(iota(0) == iota(1), 1.0, 0.0)
    upper = [a[i * 8 : (i + 1) * 8] for i in range(blocks)]
    inverse = [eye[i * 8 : (i + 1) * 8] for i in range(blocks)]
    for s in range(0, TILE, 4):
        b, r = s // 8, s % 8
        c = [lane(upper[b], s + k) for k in range(4)]
        a00, a01, a02, a03 = (every(c[k], r) for k in range(4))
        a11, a12, a13 = (every(c[k], r + 1) for k in range(1, 4))
        a22, a23 = (every(c[k], r + 2) for k in range(2, 4))
        a33 = every(c[3], r + 3)
        det = reciprocal(a00 * a11 - a01 * a01)
        p00, p01, p11 = a11 * det, -a01 * det, a00 * det
        t20, t21 = a02 * p00 + a12 * p01, a02 * p01 + a12 * p11
        t30, t31 = a03 * p00 + a13 * p01, a03 * p01 + a13 * p11
        r22 = a22 - t20 * a02 - t21 * a12
        r23 = a23 - t20 * a03 - t21 * a13
        r33 = a33 - t30 * a03 - t31 * a13
        det = reciprocal(r22 * r33 - r23 * r23)
        i22, i23, i33 = r33 * det, -r23 * det, r22 * det
        ratio1 = a01 * reciprocal(a00)
        ratio3 = r23 * reciprocal(r22)
        for strips in (upper, inverse):
            u = [every(strips[b], r + k) for k in range(4)]
            l2 = u[2] - t20 * u[0] - t21 * u[1]
            l3 = u[3] - t30 * u[0] - t31 * u[1]
            w2 = i22 * l2 + i23 * l3
            w3 = i23 * l2 + i33 * l3
            w0 = p00 * u[0] + p01 * u[1] - t20 * w2 - t30 * w3
            w1 = p01 * u[0] + p11 * u[1] - t21 * w2 - t31 * w3
            one = strips[b]
            one = jnp.where(sub == r + 1, u[1] - ratio1 * u[0], one)
            one = jnp.where(sub == r + 2, l2, one)
            one = jnp.where(sub == r + 3, l3 - ratio3 * l2, one)
            if r == 0:
                after = strips[b] - c[0] * w0 - c[1] * w1 - c[2] * w2 - c[3] * w3
                one = jnp.where(sub > 3, after, one)
            if strips is upper:
                rows = [[lane(upper[i], s + k) for k in range(4)] for i in range(b + 1, blocks)]
            strips[b] = one
            for i in range(b + 1, blocks):
                e = rows[i - b - 1]
                strips[i] = strips[i] - e[0] * w0 - e[1] * w1 - e[2] * w2 - e[3] * w3
    u = jnp.concatenate(upper, axis=0)
    inv = jnp.concatenate(inverse, axis=0)
    diagonal = jnp.sum(jnp.where(iota(0) == iota(1), u, 0.0), axis=1, keepdims=True)
    root = lax.rsqrt(diagonal)
    u = jnp.where(iota(1) >= iota(0), u * root, 0.0)
    return u.T, inv * root


def factor_corner(early, corner, lower, inverse, work, inv, between, middle, after):
    def tile(i, j):
        return corner[j, i].astype(F32)

    one = early[...].astype(F32)
    work[0] = (one + one.T) * 0.5
    lower[...] = jnp.zeros_like(lower)

    def panel(j, carry):
        between(j)
        pivot, pivot_inv = factor_tile(work[j * 5])
        lower[j * 5] = pivot
        inv[j * 5] = pivot_inv

        @pl.when(j == 0)
        def _():
            middle()
            for i in range(1, 4):
                for k in range(i + 1):
                    one = tile(i, k)
                    work[i * 4 + k] = (one + tile(k, i).T) * 0.5 if i // 2 == k // 2 else one

        def solve(i, carry):
            lower[i * 4 + j] = mm_nt(work[i * 4 + j], pivot_inv)
            return carry

        lax.fori_loop(j + 1, 4, solve, 0)

        def update_row(i, carry):
            def update(k, carry):
                work[i * 4 + k] -= mm_nt(lower[i * 4 + j], lower[k * 4 + j])
                return carry

            return lax.fori_loop(j + 1, i + 1, update, carry)

        lax.fori_loop(j + 1, 4, update_row, 0)
        return carry

    lax.fori_loop(0, 4, panel, 0)
    after()
    inverse[...] = jnp.zeros_like(inverse)
    for j in range(4):
        column = {j: inv[j * 5]}
        for i in range(j + 1, 4):
            total = mm(lower[i * 4 + j], column[j])
            for k in range(j + 1, i):
                total = total + mm(lower[i * 4 + k], column[k])
            column[i] = -mm(inv[i * 5], total)
        for i in range(j, 4):
            block = column[i].T.astype(BF16)
            inverse[j * TILE : (j + 1) * TILE, i * TILE : (i + 1) * TILE] = block


ABSENT = DEVICES * 2


def index_kernel(targets, where, row_from, col_from, seen):
    p = where[0]
    q = where[1]

    def clear_rows(i, carry):
        row_from[i] = ABSENT
        return carry

    def clear_cols(i, carry):
        col_from[i] = ABSENT
        return carry

    lax.fori_loop(0, 48, clear_rows, 0)
    lax.fori_loop(0, 16, clear_cols, 0)
    for c in range(2):
        for d in range(ROWS):
            seen[d] = 0

        def visit_row(t, carry):
            goal = targets[c, t]

            @pl.when(lax.rem(goal, ROWS) == p)
            def _():
                source = lax.rem(t, ROWS)
                row_from[c * 24 + goal // ROWS] = source * COLS * 2 + seen[source]
                seen[source] = seen[source] + 1

            return carry

        lax.fori_loop(0, 128, visit_row, 0)

        def visit_col(t, carry):
            goal = targets[c, t]

            @pl.when(lax.rem(goal, COLS) == q)
            def _():
                col_from[c * 8 + goal // COLS] = lax.rem(t, COLS) * 2

            return carry

        lax.fori_loop(0, 64, visit_col, 0)


def index_tiles(targets, where):
    return pl.pallas_call(
        index_kernel,
        out_shape=(
            jax.ShapeDtypeStruct((48,), jnp.int32),
            jax.ShapeDtypeStruct((16,), jnp.int32),
        ),
        in_specs=[spec(pltpu.SMEM), spec(pltpu.SMEM)],
        out_specs=(spec(pltpu.SMEM), spec(pltpu.SMEM)),
        scratch_shapes=[pltpu.SMEM((ROWS,), jnp.int32)],
        cost_estimate=pl.CostEstimate(flops=2**20, bytes_accessed=2**16, transcendentals=0),
        name="index",
    )(targets, where)


def column_kernel(row_from, col_from, where, front, arrived, column, heads, held, landed):
    @pl.when(where[1] < 4)
    def _():
        slots = []
        for c in range(2):
            for l in range(24):
                i = c * 24 + l
                slot = row_from[i] + col_from[c * 8]
                slots.append(slot)

                @pl.when(slot < ABSENT)
                def _(i=i, slot=slot):
                    pltpu.make_async_copy(arrived.at[slot], held.at[i], landed.at[i]).start()

        for l in range(24):
            total = front[l * TILE : (l + 1) * TILE, :].astype(F32)
            for i in (l, 24 + l):

                @pl.when(slots[i] < ABSENT)
                def _(i=i):
                    pltpu.make_async_copy(held.at[i], held.at[i], landed.at[i]).wait()

                total = total + jnp.where(slots[i] < ABSENT, held[i].astype(F32), 0.0)
            column[l] = total.astype(BF16)
            if l < 16:
                heads[l % 2, l // 2] = total.astype(BF16)


def first_column(row_from, col_from, where, front, arrived):
    return pl.pallas_call(
        column_kernel,
        out_shape=(
            jax.ShapeDtypeStruct((24, TILE, TILE), BF16),
            jax.ShapeDtypeStruct((2, 8, TILE, TILE), BF16),
        ),
        grid=(1,),
        in_specs=[
            spec(pltpu.SMEM),
            spec(pltpu.SMEM),
            spec(pltpu.SMEM),
            pl.BlockSpec((24 * TILE, TILE), lambda i: (0, 0)),
            spec(pl.ANY),
        ],
        out_specs=(
            pl.BlockSpec((24, TILE, TILE), lambda i: (0, 0, 0)),
            pl.BlockSpec((2, 8, TILE, TILE), lambda i: (0, 0, 0, 0)),
        ),
        scratch_shapes=[
            pltpu.VMEM((48, TILE, TILE), BF16),
            pltpu.SemaphoreType.DMA((48,)),
        ],
        compiler_params=pltpu.CompilerParams(vmem_limit_bytes=10 * 2**20),
        cost_estimate=pl.CostEstimate(flops=2**20, bytes_accessed=2**22, transcendentals=0),
        name="column",
    )(row_from, col_from, where, front, arrived)


def spread_kernel(
    column,
    heads,
    rows,
    cols,
    lower,
    inverse,
    early,
    corner,
    work,
    inv,
    sends,
    recvs,
    share_sends,
    share_recvs,
    corner_sends,
    corner_recvs,
    head_sends,
    head_recvs,
    pass_sends,
    pass_recvs,
    early_sends,
    early_recvs,
    locals_,
):
    p = lax.axis_index("row")
    q = lax.axis_index("col")
    z, core = p // 2, lax.rem(p, 2)
    x, y = q // 4, lax.rem(q, 4)
    source = lax.rem(q, ROWS)
    hops = lax.rem(z + 4 - source // 2, 4)
    near = core == lax.rem(source, 2)
    sibling = (z * 2 + 1 - core, q)

    def at_x(d):
        return (p, lax.rem(x + d, 4) * 4 + y)

    def at_y(d):
        return (p, x * 4 + lax.rem(y + d, 4))

    def at_z(d):
        return (lax.rem(z + d, 4) * 2 + core, q)

    def at_row(d):
        return (lax.rem(p + d, ROWS), q)

    def at_col(d):
        return (p, lax.rem(q + d, COLS))

    barrier = pltpu.get_barrier_semaphore()
    for d in range(1, COLS):
        pl.semaphore_signal(barrier, inc=1, device_id=at_col(d), device_id_type=MESH)
    for d in range(1, ROWS):
        pl.semaphore_signal(barrier, inc=1, device_id=at_row(d), device_id_type=MESH)
    pl.semaphore_wait(barrier, COLS + ROWS - 2)

    def remote(src, dst, sent, landed, peer):
        return pltpu.make_async_remote_copy(
            src, dst, sent, landed, device_id=peer, device_id_type=MESH
        )

    def copy(part, slot, peer):
        return remote(part, part, sends.at[slot], recvs.at[slot], peer)

    def corner_copy(src, dst, sent, landed, peer):
        return remote(src, dst, corner_sends.at[sent], corner_recvs.at[landed], peer)

    def head_copy(h, f, peer):
        return remote(heads.at[h], cols.at[f], head_sends.at[h], head_recvs.at[f], peer)

    def share_copy(d):
        to = lax.rem(q + d, COLS)
        part = rows.at[y, to // 4, lax.rem(to, 4)]
        return remote(column.at[to], part, share_sends.at[d], share_recvs.at[y], at_col(d))

    def pass_copy(part, slot, peer):
        return remote(part, part, pass_sends.at[slot], pass_recvs.at[slot], peer)

    def own_copy(src, dst, slot):
        own = pltpu.make_async_copy(src, dst, locals_.at[slot])
        own.start()
        own.wait()

    def early_copy(src, sent, landed, peer):
        return remote(src, early, early_sends.at[sent], early_recvs.at[landed], peer)

    first_tile = heads.at[0, 0]

    @pl.when((p == 0) & (q == 0))
    def _():
        for d in range(1, ROWS):
            early_copy(first_tile, d - 1, 0, at_row(d)).start()
        own_copy(first_tile, early, 0)

    for r in range(4):

        @pl.when((q < 4) & (p == r))
        def _(r=r):
            for d in range(1, ROWS):
                corner_copy(first_tile, corner.at[y, r], d - 1, r, at_row(d)).start()
            own_copy(first_tile, corner.at[y, r], 0)

    @pl.when((p != 0) & (q == 0))
    def _():
        early_copy(early, 0, 0, at_row(1)).wait_recv()

    @pl.when(q == 0)
    def _():
        for d in (1, 2, 3):
            early_copy(early, 6 + d, d, at_x(d)).start()

    for r in range(4):

        @pl.when((q < 4) & (p != r))
        def _(r=r):
            corner_copy(first_tile, corner.at[y, r], 0, r, at_row(1)).wait_recv()

    @pl.when(x == 0)
    def _():
        for d in (1, 2, 3):
            corner_copy(corner.at[y], corner.at[y], 6 + d, 3 + d, at_x(d)).start()

    for d in (1, 2, 3):

        @pl.when((y == 0) & (x == d))
        def _(d=d):
            early_copy(early, 0, d, at_x(4 - d)).wait_recv()

    @pl.when(y == 0)
    def _():
        for d in (1, 2, 3):
            early_copy(early, 9 + d, 3 + d, at_y(d)).start()

    @pl.when((x == 0) & (q != p))
    def _():
        head_copy(0, y, (p, p)).start()

    @pl.when(x == 0)
    def _():
        head_copy(1, y, (p, p + 8)).start()

    @pl.when(x == 0)
    def _():
        for d in range(1, COLS):
            share_copy(d).start()
        own_copy(column.at[q], rows.at[y, 0, y], 1)

    @pl.when((x == 0) & (q == p))
    def _():
        own_copy(heads.at[0], cols.at[y], 2)

    for d in (1, 2, 3):

        @pl.when(x == d)
        def _(d=d):
            corner_copy(corner.at[y], corner.at[y], 6 + d, 3 + d, at_x(4 - d)).wait_recv()

    last = [corner_copy(corner.at[y], corner.at[y], 9 + d, 6 + d, at_y(d)) for d in (1, 2, 3)]
    for one in last:
        one.start()

    for d in (1, 2, 3):

        @pl.when(y == d)
        def _(d=d):
            early_copy(early, 0, 3 + d, at_y(4 - d)).wait_recv()

    first = []
    for d in (1, 2, 3):
        first.append(copy(rows.at[:, x, y, 0], d - 1, at_x(d)))
        first.append(copy(rows.at[:, x, y, 1], d + 2, at_y(d)))
    second = []
    for d in (1, 2, 3):
        second.append(copy(rows.at[:, :, y, 0], d + 5, at_y(d)))
        second.append(copy(rows.at[:, x, :, 1], d + 8, at_x(d)))
    low, high = cols.at[pl.ds(0, 2)], cols.at[pl.ds(2, 2)]

    def middle():
        for f in range(4):

            @pl.when(q != f)
            def _(f=f):
                part = rows.at[f, x, y]
                remote(part, part, share_sends.at[0], share_recvs.at[f], at_col(1)).wait_recv()

        for one in first:
            one.start()

        for f in range(4):

            @pl.when((p == source) & (q != f))
            def _(f=f):
                head_copy(0, f, (p, p)).wait_recv()

        @pl.when(p == source)
        def _():
            pass_copy(low, 0, at_z(1)).start()
            pass_copy(high, 1, at_z(3)).start()
            pass_copy(high, 2, at_z(1)).start()
            pass_copy(low, 3, at_z(3)).start()
            pass_copy(cols, 6, sibling).start()

        for one in last:
            one.wait_recv()

    def between(j):
        @pl.when(j == 1)
        def _():
            for one in first:
                one.wait_recv()
            for one in second:
                one.start()

        @pl.when((j == 2) & near & (hops == 1))
        def _():
            pass_copy(low, 0, at_z(3)).wait_recv()
            pass_copy(low, 4, at_z(1)).start()
            pass_copy(high, 2, at_z(3)).wait_recv()
            pass_copy(cols, 6, sibling).start()

        @pl.when((j == 2) & near & (hops == 3))
        def _():
            pass_copy(high, 1, at_z(1)).wait_recv()
            pass_copy(high, 5, at_z(3)).start()
            pass_copy(low, 3, at_z(1)).wait_recv()
            pass_copy(cols, 6, sibling).start()

    def after():
        @pl.when(near & (hops == 2))
        def _():
            pass_copy(low, 4, at_z(3)).wait_recv()
            pass_copy(high, 5, at_z(1)).wait_recv()
            pass_copy(cols, 6, sibling).start()

    factor_corner(early, corner, lower, inverse, work, inv, between, middle, after)

    for one in second:
        one.wait_recv()

    @pl.when(jnp.logical_not(near))
    def _():
        pass_copy(cols, 6, sibling).wait_recv()

    @pl.when(near)
    def _():
        pass_copy(cols, 6, sibling).wait_send()

    @pl.when(p == source)
    def _():
        pass_copy(low, 0, at_z(1)).wait_send()
        pass_copy(high, 1, at_z(3)).wait_send()
        pass_copy(high, 2, at_z(1)).wait_send()
        pass_copy(low, 3, at_z(3)).wait_send()

    @pl.when(near & (hops == 1))
    def _():
        pass_copy(low, 4, at_z(1)).wait_send()

    @pl.when(near & (hops == 3))
    def _():
        pass_copy(high, 5, at_z(3)).wait_send()

    for one in last + first + second:
        one.wait_send()

    @pl.when(x == 0)
    def _():
        for d in range(1, COLS):
            share_copy(d).wait_send()
        for d in (1, 2, 3):
            corner_copy(corner.at[y], corner.at[y], 6 + d, 3 + d, at_x(d)).wait_send()
        head_copy(1, y, (p, p + 8)).wait_send()

    @pl.when((x == 0) & (q != p))
    def _():
        head_copy(0, y, (p, p)).wait_send()

    @pl.when((q < 4) & (p < 4))
    def _():
        for d in range(1, ROWS):
            corner_copy(first_tile, early, d - 1, 0, at_row(d)).wait_send()

    @pl.when((p == 0) & (q == 0))
    def _():
        for d in range(1, ROWS):
            early_copy(first_tile, d - 1, 0, at_row(d)).wait_send()

    @pl.when(q == 0)
    def _():
        for d in (1, 2, 3):
            early_copy(early, 6 + d, d, at_x(d)).wait_send()

    @pl.when(y == 0)
    def _():
        for d in (1, 2, 3):
            early_copy(early, 9 + d, 3 + d, at_y(d)).wait_send()


def spread_panels(column, heads):
    return pl.pallas_call(
        spread_kernel,
        out_shape=(
            jax.ShapeDtypeStruct((4, 4, 4, 2, 96, TILE), BF16),
            jax.ShapeDtypeStruct((4, 8, TILE, TILE), BF16),
            jax.ShapeDtypeStruct((16, TILE, TILE), F32),
            jax.ShapeDtypeStruct((4 * TILE, 4 * TILE), BF16),
        ),
        in_specs=[spec(pltpu.VMEM)] * 2,
        out_specs=(spec(pltpu.VMEM),) * 4,
        scratch_shapes=[
            pltpu.VMEM((TILE, TILE), BF16),
            pltpu.VMEM((4, 4, TILE, TILE), BF16),
            pltpu.VMEM((16, TILE, TILE), F32),
            pltpu.VMEM((16, TILE, TILE), F32),
            pltpu.SemaphoreType.DMA((12,)),
            pltpu.SemaphoreType.DMA((12,)),
            pltpu.SemaphoreType.DMA((COLS,)),
            pltpu.SemaphoreType.DMA((4,)),
            pltpu.SemaphoreType.DMA((13,)),
            pltpu.SemaphoreType.DMA((10,)),
            pltpu.SemaphoreType.DMA((2,)),
            pltpu.SemaphoreType.DMA((4,)),
            pltpu.SemaphoreType.DMA((7,)),
            pltpu.SemaphoreType.DMA((7,)),
            pltpu.SemaphoreType.DMA((13,)),
            pltpu.SemaphoreType.DMA((7,)),
            pltpu.SemaphoreType.DMA((3,)),
        ],
        compiler_params=pltpu.CompilerParams(
            collective_id=2, has_side_effects=True, vmem_limit_bytes=20 * 2**20
        ),
        cost_estimate=pl.CostEstimate(flops=2**30, bytes_accessed=2**23, transcendentals=0),
        name="spread",
    )(column, heads)


def finish_kernel(
    row_from,
    col_from,
    where,
    front,
    arrived,
    rows,
    cols,
    lower,
    inverse,
    out,
    factor_cols,
    solved,
    live,
    held,
    landed,
):
    g = pl.program_id(0)
    p = where[0]
    q = where[1]
    chunks = [pl.ds(i * 32, 32) for i in range(8)]

    @pl.when(g == 0)
    def _():
        for i, at in enumerate(chunks):
            pltpu.make_async_copy(arrived.at[at], held.at[at], landed.at[i]).start()
        held[ABSENT] = jnp.zeros((TILE, TILE), BF16)
        for m in range(8):
            wide = jnp.concatenate([cols[f, m] for f in range(4)], axis=1)
            found = jnp.dot(wide, inverse[...], preferred_element_type=F32)
            factor_cols[:, m * TILE : (m + 1) * TILE] = found.astype(BF16).T

    wide = jnp.concatenate(
        [rows[f] for f in range(4)], axis=1
    )
    found = jnp.dot(wide, inverse[...], preferred_element_type=F32)
    solved[...] = found
    live[...] = found.astype(BF16)

    @pl.when((g == 0) & (p < 4))
    def _():
        for f in range(4):
            tile = lower[p * 4 + f]
            at = slice(f * TILE, (f + 1) * TILE)
            solved[:TILE, at] = tile
            live[:TILE, at] = jnp.where(f // 2 < p // 2, tile, 0.0).astype(BF16)

    @pl.when(g == 0)
    def _():
        for i, at in enumerate(chunks):
            pltpu.make_async_copy(arrived.at[at], held.at[at], landed.at[i]).wait()

    for pair in range(4):
        at = slice(pair * 256, (pair + 1) * 256)
        product = jnp.dot(live[...], factor_cols[:, at], preferred_element_type=F32)
        for t in range(3):
            for m in (pair * 2, pair * 2 + 1):
                down = slice(t * TILE, (t + 1) * TILE)
                across = slice(m * TILE, (m + 1) * TILE)
                total = front[down, across].astype(F32)
                for c in range(2):
                    slot = row_from[c * 24 + g * 3 + t] + col_from[c * 8 + m]
                    total = total + held[jnp.minimum(slot, ABSENT)].astype(F32)
                out[down, across] = total - product[down, (m % 2) * TILE : (m % 2 + 1) * TILE]

    for f in range(4):

        @pl.when(q == f)
        def _(f=f):
            out[:, :TILE] = solved[:, f * TILE : (f + 1) * TILE]


def finish(row_from, col_from, where, front, arrived, rows, cols, lower, inverse):
    return pl.pallas_call(
        finish_kernel,
        out_shape=jax.ShapeDtypeStruct((24 * TILE, 8 * TILE), F32),
        grid=(8,),
        in_specs=[
            spec(pltpu.SMEM),
            spec(pltpu.SMEM),
            spec(pltpu.SMEM),
            pl.BlockSpec((3 * TILE, 8 * TILE), lambda g: (g, 0)),
            spec(pl.ANY),
            pl.BlockSpec((4, 3 * TILE, TILE), lambda g: (0, g, 0)),
            spec(pltpu.VMEM),
            spec(pltpu.VMEM),
            spec(pltpu.VMEM),
        ],
        out_specs=pl.BlockSpec((3 * TILE, 8 * TILE), lambda g: (g, 0)),
        scratch_shapes=[
            pltpu.VMEM((4 * TILE, 8 * TILE), BF16),
            pltpu.VMEM((3 * TILE, 4 * TILE), F32),
            pltpu.VMEM((3 * TILE, 4 * TILE), BF16),
            pltpu.VMEM((ABSENT + 1, TILE, TILE), BF16),
            pltpu.SemaphoreType.DMA((8,)),
        ],
        compiler_params=pltpu.CompilerParams(vmem_limit_bytes=28 * 2**20),
        cost_estimate=pl.CostEstimate(flops=2**33, bytes_accessed=32 * 2**20, transcendentals=0),
        name="finish",
    )(row_from, col_from, where, front, arrived, rows, cols, lower, inverse)


def shards(front_block, child_blocks, row_offsets, tile_targets):
    where = jnp.stack([lax.axis_index("row"), lax.axis_index("col")]).astype(jnp.int32)
    picked = place(tile_targets, where, row_offsets, child_blocks)
    arrived = lax.all_to_all(
        picked.reshape(DEVICES, 2, TILE, TILE), ("row", "col"), 0, 0, tiled=True
    ).reshape(DEVICES * 2, TILE, TILE)
    row_from, col_from = index_tiles(tile_targets, where)
    column, heads = first_column(row_from, col_from, where, front_block, arrived)
    rows, cols, lower, inverse = spread_panels(
        column.reshape(COLS, 2, 96, TILE), heads
    )
    rows = rows.reshape(4, 24 * TILE, TILE)
    return finish(row_from, col_from, where, front_block, arrived, rows, cols, lower, inverse)


def solution(mesh):
    return jax.shard_map(
        shards,
        mesh=mesh,
        in_specs=(P("row", "col"), P(None, "row", "col"), P(), P()),
        out_specs=P("row", "col"),
        check_vma=False,
    )
```

```python
import jax
import jax.numpy as jnp
from jax import lax
from jax.experimental import pallas as pl
from jax.experimental.pallas import tpu as pltpu
from jax.sharding import PartitionSpec as P

TILE = 128
ROWS = 8
COLS = 16
DEVICES = ROWS * COLS
MESH = pl.DeviceIdType.MESH
BF16 = jnp.bfloat16
F32 = jnp.float32
NT = (((1,), (1,)), ((), ()))


def spec(space):
    return pl.BlockSpec(memory_space=space)


def iota(dim):
    return lax.broadcasted_iota(jnp.int32, (TILE, TILE), dim)


def one_hot(offsets):
    return jnp.where(iota(0) == offsets, 1.0, 0.0).astype(BF16)


def place_kernel(targets, where, offsets, child, picked, shifted, tiles, rank, seen, sent):
    c = pl.program_id(0)
    p = where[0]
    q = where[1]

    for d in range(ROWS):
        seen[d] = 0

    def order(l, carry):
        owner = lax.rem(targets[c, l * ROWS + p], ROWS)
        rank[l] = owner * COLS * 2 + seen[owner]
        seen[owner] = seen[owner] + 1
        return carry

    lax.fori_loop(0, 16, order, 0)

    def tile_offsets(t):
        both = offsets[:, pl.ds(pl.multiple_of(t * TILE, TILE), TILE)]
        return jnp.where(c == 0, both[:1], both[1:])

    for l in range(16):
        hot = one_hot(tile_offsets(l * ROWS + p))
        moved = jnp.dot(
            hot, child[0, l * TILE : (l + 1) * TILE, :], preferred_element_type=F32
        )
        shifted[l * TILE : (l + 1) * TILE, :] = moved.astype(BF16)
    for k in range(4):
        hot = one_hot(tile_offsets(k * COLS + q)).T
        front_col = targets[c, k * COLS + q]
        base = lax.rem(front_col, COLS) * 2
        for part in range(4):
            rows = shifted[part * 512 : (part + 1) * 512, k * TILE : (k + 1) * TILE]
            placed = jnp.dot(rows, hot, preferred_element_type=F32)
            for s in range(4):
                l = part * 4 + s
                tile = placed[s * TILE : (s + 1) * TILE]
                held = tiles.at[(c * 4 + k) * 16 + l]
                held[...] = tile.astype(BF16)
                pltpu.make_async_copy(held, picked.at[rank[l] + base], sent).start()

    @pl.when(c == 1)
    def _():
        pltpu.make_async_copy(tiles, tiles, sent).wait()


def place(targets, where, offsets, child):
    return pl.pallas_call(
        place_kernel,
        out_shape=jax.ShapeDtypeStruct((DEVICES * 2, TILE, TILE), BF16),
        grid=(2,),
        in_specs=[
            spec(pltpu.SMEM),
            spec(pltpu.SMEM),
            spec(pltpu.VMEM),
            pl.BlockSpec((1, 16 * TILE, 4 * TILE), lambda c: (c, 0, 0)),
        ],
        out_specs=spec(pl.ANY),
        scratch_shapes=[
            pltpu.VMEM((16 * TILE, 4 * TILE), BF16),
            pltpu.VMEM((DEVICES, TILE, TILE), BF16),
            pltpu.SMEM((16,), jnp.int32),
            pltpu.SMEM((ROWS,), jnp.int32),
            pltpu.SemaphoreType.DMA,
        ],
        compiler_params=pltpu.CompilerParams(vmem_limit_bytes=56 * 2**20),
        cost_estimate=pl.CostEstimate(flops=2**31, bytes_accessed=14 * 2**20, transcendentals=0),
        name="place",
    )(targets, where, offsets, child)


def mm(a, b):
    return jnp.dot(a, b, precision=lax.Precision.HIGHEST, preferred_element_type=F32)


def mm_nt(a, b):
    return lax.dot_general(
        a, b, NT, precision=lax.Precision.HIGHEST, preferred_element_type=F32
    )


def reciprocal(x):
    r = pl.reciprocal(x, approx=True)
    r = r * (2.0 - x * r)
    return r * (2.0 - x * r)


def lane(x, s):
    return jnp.take_along_axis(x, jnp.full((8, TILE), s, jnp.int32), axis=1)


def every(x, r):
    return jnp.broadcast_to(x[r : r + 1], (8, TILE))


def factor_tile(a):
    blocks = TILE // 8
    sub = lax.broadcasted_iota(jnp.int32, (8, TILE), 0)
    eye = jnp.where(iota(0) == iota(1), 1.0, 0.0)
    upper = [a[i * 8 : (i + 1) * 8] for i in range(blocks)]
    inverse = [eye[i * 8 : (i + 1) * 8] for i in range(blocks)]
    for s in range(0, TILE, 4):
        b, r = s // 8, s % 8
        c = [lane(upper[b], s + k) for k in range(4)]
        a00, a01, a02, a03 = (every(c[k], r) for k in range(4))
        a11, a12, a13 = (every(c[k], r + 1) for k in range(1, 4))
        a22, a23 = (every(c[k], r + 2) for k in range(2, 4))
        a33 = every(c[3], r + 3)
        det = reciprocal(a00 * a11 - a01 * a01)
        p00, p01, p11 = a11 * det, -a01 * det, a00 * det
        t20, t21 = a02 * p00 + a12 * p01, a02 * p01 + a12 * p11
        t30, t31 = a03 * p00 + a13 * p01, a03 * p01 + a13 * p11
        r22 = a22 - t20 * a02 - t21 * a12
        r23 = a23 - t20 * a03 - t21 * a13
        r33 = a33 - t30 * a03 - t31 * a13
        det = reciprocal(r22 * r33 - r23 * r23)
        i22, i23, i33 = r33 * det, -r23 * det, r22 * det
        ratio1 = a01 * reciprocal(a00)
        ratio3 = r23 * reciprocal(r22)
        for strips in (upper, inverse):
            u = [every(strips[b], r + k) for k in range(4)]
            l2 = u[2] - t20 * u[0] - t21 * u[1]
            l3 = u[3] - t30 * u[0] - t31 * u[1]
            w2 = i22 * l2 + i23 * l3
            w3 = i23 * l2 + i33 * l3
            w0 = p00 * u[0] + p01 * u[1] - t20 * w2 - t30 * w3
            w1 = p01 * u[0] + p11 * u[1] - t21 * w2 - t31 * w3
            one = strips[b]
            one = jnp.where(sub == r + 1, u[1] - ratio1 * u[0], one)
            one = jnp.where(sub == r + 2, l2, one)
            one = jnp.where(sub == r + 3, l3 - ratio3 * l2, one)
            if r == 0:
                after = strips[b] - c[0] * w0 - c[1] * w1 - c[2] * w2 - c[3] * w3
                one = jnp.where(sub > 3, after, one)
            if strips is upper:
                rows = [[lane(upper[i], s + k) for k in range(4)] for i in range(b + 1, blocks)]
            strips[b] = one
            for i in range(b + 1, blocks):
                e = rows[i - b - 1]
                strips[i] = strips[i] - e[0] * w0 - e[1] * w1 - e[2] * w2 - e[3] * w3
    u = jnp.concatenate(upper, axis=0)
    inv = jnp.concatenate(inverse, axis=0)
    diagonal = jnp.sum(jnp.where(iota(0) == iota(1), u, 0.0), axis=1, keepdims=True)
    root = lax.rsqrt(diagonal)
    u = jnp.where(iota(1) >= iota(0), u * root, 0.0)
    return u.T, inv * root


def factor_corner(early, corner, lower, inverse, work, inv, between, middle, after):
    def tile(i, j):
        return corner[j, i].astype(F32)

    one = early[...].astype(F32)
    work[0] = (one + one.T) * 0.5
    lower[...] = jnp.zeros_like(lower)

    def panel(j, carry):
        between(j)
        pivot, pivot_inv = factor_tile(work[j * 5])
        lower[j * 5] = pivot
        inv[j * 5] = pivot_inv

        @pl.when(j == 0)
        def _():
            middle()
            for i in range(1, 4):
                for k in range(i + 1):
                    one = tile(i, k)
                    work[i * 4 + k] = (one + tile(k, i).T) * 0.5 if i // 2 == k // 2 else one

        def solve(i, carry):
            lower[i * 4 + j] = mm_nt(work[i * 4 + j], pivot_inv)
            return carry

        lax.fori_loop(j + 1, 4, solve, 0)

        def update_row(i, carry):
            def update(k, carry):
                work[i * 4 + k] -= mm_nt(lower[i * 4 + j], lower[k * 4 + j])
                return carry

            return lax.fori_loop(j + 1, i + 1, update, carry)

        lax.fori_loop(j + 1, 4, update_row, 0)
        return carry

    lax.fori_loop(0, 4, panel, 0)
    after()
    inverse[...] = jnp.zeros_like(inverse)
    for j in range(4):
        column = {j: inv[j * 5]}
        for i in range(j + 1, 4):
            total = mm(lower[i * 4 + j], column[j])
            for k in range(j + 1, i):
                total = total + mm(lower[i * 4 + k], column[k])
            column[i] = -mm(inv[i * 5], total)
        for i in range(j, 4):
            block = column[i].T.astype(BF16)
            inverse[j * TILE : (j + 1) * TILE, i * TILE : (i + 1) * TILE] = block


ABSENT = DEVICES * 2


def index_kernel(targets, where, row_from, col_from, seen):
    p = where[0]
    q = where[1]

    def clear_rows(i, carry):
        row_from[i] = ABSENT
        return carry

    def clear_cols(i, carry):
        col_from[i] = ABSENT
        return carry

    lax.fori_loop(0, 48, clear_rows, 0)
    lax.fori_loop(0, 16, clear_cols, 0)
    for c in range(2):
        for d in range(ROWS):
            seen[d] = 0

        def visit_row(t, carry):
            goal = targets[c, t]

            @pl.when(lax.rem(goal, ROWS) == p)
            def _():
                source = lax.rem(t, ROWS)
                row_from[c * 24 + goal // ROWS] = source * COLS * 2 + seen[source]
                seen[source] = seen[source] + 1

            return carry

        lax.fori_loop(0, 128, visit_row, 0)

        def visit_col(t, carry):
            goal = targets[c, t]

            @pl.when(lax.rem(goal, COLS) == q)
            def _():
                col_from[c * 8 + goal // COLS] = lax.rem(t, COLS) * 2

            return carry

        lax.fori_loop(0, 64, visit_col, 0)


def index_tiles(targets, where):
    return pl.pallas_call(
        index_kernel,
        out_shape=(
            jax.ShapeDtypeStruct((48,), jnp.int32),
            jax.ShapeDtypeStruct((16,), jnp.int32),
        ),
        in_specs=[spec(pltpu.SMEM), spec(pltpu.SMEM)],
        out_specs=(spec(pltpu.SMEM), spec(pltpu.SMEM)),
        scratch_shapes=[pltpu.SMEM((ROWS,), jnp.int32)],
        cost_estimate=pl.CostEstimate(flops=2**20, bytes_accessed=2**16, transcendentals=0),
        name="index",
    )(targets, where)


def column_kernel(row_from, col_from, where, front, arrived, column, heads, held, landed):
    @pl.when(where[1] < 4)
    def _():
        slots = []
        for c in range(2):
            for l in range(24):
                i = c * 24 + l
                slot = row_from[i] + col_from[c * 8]
                slots.append(slot)

                @pl.when(slot < ABSENT)
                def _(i=i, slot=slot):
                    pltpu.make_async_copy(arrived.at[slot], held.at[i], landed.at[i]).start()

        for l in range(24):
            total = front[l * TILE : (l + 1) * TILE, :].astype(F32)
            for i in (l, 24 + l):

                @pl.when(slots[i] < ABSENT)
                def _(i=i):
                    pltpu.make_async_copy(held.at[i], held.at[i], landed.at[i]).wait()

                total = total + jnp.where(slots[i] < ABSENT, held[i].astype(F32), 0.0)
            column[l] = total.astype(BF16)
            if l < 16:
                heads[l % 2, l // 2] = total.astype(BF16)


def first_column(row_from, col_from, where, front, arrived):
    return pl.pallas_call(
        column_kernel,
        out_shape=(
            jax.ShapeDtypeStruct((24, TILE, TILE), BF16),
            jax.ShapeDtypeStruct((2, 8, TILE, TILE), BF16),
        ),
        grid=(1,),
        in_specs=[
            spec(pltpu.SMEM),
            spec(pltpu.SMEM),
            spec(pltpu.SMEM),
            pl.BlockSpec((24 * TILE, TILE), lambda i: (0, 0)),
            spec(pl.ANY),
        ],
        out_specs=(
            pl.BlockSpec((24, TILE, TILE), lambda i: (0, 0, 0)),
            pl.BlockSpec((2, 8, TILE, TILE), lambda i: (0, 0, 0, 0)),
        ),
        scratch_shapes=[
            pltpu.VMEM((48, TILE, TILE), BF16),
            pltpu.SemaphoreType.DMA((48,)),
        ],
        compiler_params=pltpu.CompilerParams(vmem_limit_bytes=52 * 2**20),
        cost_estimate=pl.CostEstimate(flops=2**20, bytes_accessed=2**22, transcendentals=0),
        name="column",
    )(row_from, col_from, where, front, arrived)


def spread_kernel(
    column,
    heads,
    rows,
    cols,
    lower,
    inverse,
    early,
    corner,
    work,
    inv,
    sends,
    recvs,
    share_sends,
    share_recvs,
    corner_sends,
    corner_recvs,
    head_sends,
    head_recvs,
    pass_sends,
    pass_recvs,
    early_sends,
    early_recvs,
    locals_,
):
    p = lax.axis_index("row")
    q = lax.axis_index("col")
    z, core = p // 2, lax.rem(p, 2)
    x, y = q // 4, lax.rem(q, 4)
    source = lax.rem(q, ROWS)
    hops = lax.rem(z + 4 - source // 2, 4)
    near = core == lax.rem(source, 2)
    sibling = (z * 2 + 1 - core, q)

    def at_x(d):
        return (p, lax.rem(x + d, 4) * 4 + y)

    def at_y(d):
        return (p, x * 4 + lax.rem(y + d, 4))

    def at_z(d):
        return (lax.rem(z + d, 4) * 2 + core, q)

    def at_row(d):
        return (lax.rem(p + d, ROWS), q)

    def at_col(d):
        return (p, lax.rem(q + d, COLS))

    barrier = pltpu.get_barrier_semaphore()
    for d in range(1, COLS):
        pl.semaphore_signal(barrier, inc=1, device_id=at_col(d), device_id_type=MESH)
    for d in range(1, ROWS):
        pl.semaphore_signal(barrier, inc=1, device_id=at_row(d), device_id_type=MESH)
    pl.semaphore_wait(barrier, COLS + ROWS - 2)

    def remote(src, dst, sent, landed, peer):
        return pltpu.make_async_remote_copy(
            src, dst, sent, landed, device_id=peer, device_id_type=MESH
        )

    def copy(part, slot, peer):
        return remote(part, part, sends.at[slot], recvs.at[slot], peer)

    def corner_copy(src, dst, sent, landed, peer):
        return remote(src, dst, corner_sends.at[sent], corner_recvs.at[landed], peer)

    def head_copy(h, f, peer):
        return remote(heads.at[h], cols.at[f], head_sends.at[h], head_recvs.at[f], peer)

    def share_copy(d):
        to = lax.rem(q + d, COLS)
        part = rows.at[y, to // 4, lax.rem(to, 4)]
        return remote(column.at[to], part, share_sends.at[d], share_recvs.at[y], at_col(d))

    def pass_copy(part, slot, peer):
        return remote(part, part, pass_sends.at[slot], pass_recvs.at[slot], peer)

    def own_copy(src, dst, slot):
        own = pltpu.make_async_copy(src, dst, locals_.at[slot])
        own.start()
        own.wait()

    def early_copy(src, sent, landed, peer):
        return remote(src, early, early_sends.at[sent], early_recvs.at[landed], peer)

    first_tile = heads.at[0, 0]

    @pl.when((p == 0) & (q == 0))
    def _():
        for d in range(1, ROWS):
            early_copy(first_tile, d - 1, 0, at_row(d)).start()
        own_copy(first_tile, early, 0)

    for r in range(4):

        @pl.when((q < 4) & (p == r))
        def _(r=r):
            for d in range(1, ROWS):
                corner_copy(first_tile, corner.at[y, r], d - 1, r, at_row(d)).start()
            own_copy(first_tile, corner.at[y, r], 0)

    @pl.when((p != 0) & (q == 0))
    def _():
        early_copy(early, 0, 0, at_row(1)).wait_recv()

    @pl.when(q == 0)
    def _():
        for d in (1, 2, 3):
            early_copy(early, 6 + d, d, at_x(d)).start()

    for r in range(4):

        @pl.when((q < 4) & (p != r))
        def _(r=r):
            corner_copy(first_tile, corner.at[y, r], 0, r, at_row(1)).wait_recv()

    @pl.when(x == 0)
    def _():
        for d in (1, 2, 3):
            corner_copy(corner.at[y], corner.at[y], 6 + d, 3 + d, at_x(d)).start()

    for d in (1, 2, 3):

        @pl.when((y == 0) & (x == d))
        def _(d=d):
            early_copy(early, 0, d, at_x(4 - d)).wait_recv()

    @pl.when(y == 0)
    def _():
        for d in (1, 2, 3):
            early_copy(early, 9 + d, 3 + d, at_y(d)).start()

    @pl.when((x == 0) & (q != p))
    def _():
        head_copy(0, y, (p, p)).start()

    @pl.when(x == 0)
    def _():
        head_copy(1, y, (p, p + 8)).start()

    @pl.when(x == 0)
    def _():
        for d in range(1, COLS):
            share_copy(d).start()
        own_copy(column.at[q], rows.at[y, 0, y], 1)

    @pl.when((x == 0) & (q == p))
    def _():
        own_copy(heads.at[0], cols.at[y], 2)

    for d in (1, 2, 3):

        @pl.when(x == d)
        def _(d=d):
            corner_copy(corner.at[y], corner.at[y], 6 + d, 3 + d, at_x(4 - d)).wait_recv()

    last = [corner_copy(corner.at[y], corner.at[y], 9 + d, 6 + d, at_y(d)) for d in (1, 2, 3)]
    for one in last:
        one.start()

    for d in (1, 2, 3):

        @pl.when(y == d)
        def _(d=d):
            early_copy(early, 0, 3 + d, at_y(4 - d)).wait_recv()

    first = []
    for d in (1, 2, 3):
        first.append(copy(rows.at[:, x, y, 0], d - 1, at_x(d)))
        first.append(copy(rows.at[:, x, y, 1], d + 2, at_y(d)))
    second = []
    for d in (1, 2, 3):
        second.append(copy(rows.at[:, :, y, 0], d + 5, at_y(d)))
        second.append(copy(rows.at[:, x, :, 1], d + 8, at_x(d)))
    low, high = cols.at[pl.ds(0, 2)], cols.at[pl.ds(2, 2)]

    def middle():
        for f in range(4):

            @pl.when(q != f)
            def _(f=f):
                part = rows.at[f, x, y]
                remote(part, part, share_sends.at[0], share_recvs.at[f], at_col(1)).wait_recv()

        for one in first:
            one.start()

        for f in range(4):

            @pl.when((p == source) & (q != f))
            def _(f=f):
                head_copy(0, f, (p, p)).wait_recv()

        @pl.when(p == source)
        def _():
            pass_copy(low, 0, at_z(1)).start()
            pass_copy(high, 1, at_z(3)).start()
            pass_copy(high, 2, at_z(1)).start()
            pass_copy(low, 3, at_z(3)).start()
            pass_copy(cols, 6, sibling).start()

        for one in last:
            one.wait_recv()

    def between(j):
        @pl.when(j == 1)
        def _():
            for one in first:
                one.wait_recv()
            for one in second:
                one.start()

        @pl.when((j == 2) & near & (hops == 1))
        def _():
            pass_copy(low, 0, at_z(3)).wait_recv()
            pass_copy(low, 4, at_z(1)).start()
            pass_copy(high, 2, at_z(3)).wait_recv()
            pass_copy(cols, 6, sibling).start()

        @pl.when((j == 2) & near & (hops == 3))
        def _():
            pass_copy(high, 1, at_z(1)).wait_recv()
            pass_copy(high, 5, at_z(3)).start()
            pass_copy(low, 3, at_z(1)).wait_recv()
            pass_copy(cols, 6, sibling).start()

    def after():
        @pl.when(near & (hops == 2))
        def _():
            pass_copy(low, 4, at_z(3)).wait_recv()
            pass_copy(high, 5, at_z(1)).wait_recv()
            pass_copy(cols, 6, sibling).start()

    factor_corner(early, corner, lower, inverse, work, inv, between, middle, after)

    for one in second:
        one.wait_recv()

    @pl.when(jnp.logical_not(near))
    def _():
        pass_copy(cols, 6, sibling).wait_recv()

    @pl.when(near)
    def _():
        pass_copy(cols, 6, sibling).wait_send()

    @pl.when(p == source)
    def _():
        pass_copy(low, 0, at_z(1)).wait_send()
        pass_copy(high, 1, at_z(3)).wait_send()
        pass_copy(high, 2, at_z(1)).wait_send()
        pass_copy(low, 3, at_z(3)).wait_send()

    @pl.when(near & (hops == 1))
    def _():
        pass_copy(low, 4, at_z(1)).wait_send()

    @pl.when(near & (hops == 3))
    def _():
        pass_copy(high, 5, at_z(3)).wait_send()

    for one in last + first + second:
        one.wait_send()

    @pl.when(x == 0)
    def _():
        for d in range(1, COLS):
            share_copy(d).wait_send()
        for d in (1, 2, 3):
            corner_copy(corner.at[y], corner.at[y], 6 + d, 3 + d, at_x(d)).wait_send()
        head_copy(1, y, (p, p + 8)).wait_send()

    @pl.when((x == 0) & (q != p))
    def _():
        head_copy(0, y, (p, p)).wait_send()

    @pl.when((q < 4) & (p < 4))
    def _():
        for d in range(1, ROWS):
            corner_copy(first_tile, early, d - 1, 0, at_row(d)).wait_send()

    @pl.when((p == 0) & (q == 0))
    def _():
        for d in range(1, ROWS):
            early_copy(first_tile, d - 1, 0, at_row(d)).wait_send()

    @pl.when(q == 0)
    def _():
        for d in (1, 2, 3):
            early_copy(early, 6 + d, d, at_x(d)).wait_send()

    @pl.when(y == 0)
    def _():
        for d in (1, 2, 3):
            early_copy(early, 9 + d, 3 + d, at_y(d)).wait_send()


def spread_panels(column, heads):
    return pl.pallas_call(
        spread_kernel,
        out_shape=(
            jax.ShapeDtypeStruct((4, 4, 4, 2, 96, TILE), BF16),
            jax.ShapeDtypeStruct((4, 8, TILE, TILE), BF16),
            jax.ShapeDtypeStruct((16, TILE, TILE), F32),
            jax.ShapeDtypeStruct((4 * TILE, 4 * TILE), BF16),
        ),
        in_specs=[spec(pltpu.VMEM)] * 2,
        out_specs=(spec(pltpu.VMEM),) * 4,
        scratch_shapes=[
            pltpu.VMEM((TILE, TILE), BF16),
            pltpu.VMEM((4, 4, TILE, TILE), BF16),
            pltpu.VMEM((16, TILE, TILE), F32),
            pltpu.VMEM((16, TILE, TILE), F32),
            pltpu.SemaphoreType.DMA((12,)),
            pltpu.SemaphoreType.DMA((12,)),
            pltpu.SemaphoreType.DMA((COLS,)),
            pltpu.SemaphoreType.DMA((4,)),
            pltpu.SemaphoreType.DMA((13,)),
            pltpu.SemaphoreType.DMA((10,)),
            pltpu.SemaphoreType.DMA((2,)),
            pltpu.SemaphoreType.DMA((4,)),
            pltpu.SemaphoreType.DMA((7,)),
            pltpu.SemaphoreType.DMA((7,)),
            pltpu.SemaphoreType.DMA((13,)),
            pltpu.SemaphoreType.DMA((7,)),
            pltpu.SemaphoreType.DMA((3,)),
        ],
        compiler_params=pltpu.CompilerParams(
            collective_id=2, has_side_effects=True, vmem_limit_bytes=20 * 2**20
        ),
        cost_estimate=pl.CostEstimate(flops=2**30, bytes_accessed=2**23, transcendentals=0),
        name="spread",
    )(column, heads)


def finish_kernel(
    row_from,
    col_from,
    where,
    front,
    arrived,
    rows,
    cols,
    lower,
    inverse,
    out,
    factor_cols,
    solved,
    live,
    held,
    landed,
):
    g = pl.program_id(0)
    p = where[0]
    q = where[1]
    chunks = [pl.ds(i * 32, 32) for i in range(8)]

    @pl.when(g == 0)
    def _():
        for i, at in enumerate(chunks):
            pltpu.make_async_copy(arrived.at[at], held.at[at], landed.at[i]).start()
        held[ABSENT] = jnp.zeros((TILE, TILE), BF16)
        for m in range(8):
            wide = jnp.concatenate([cols[f, m] for f in range(4)], axis=1)
            found = jnp.dot(wide, inverse[...], preferred_element_type=F32)
            factor_cols[:, m * TILE : (m + 1) * TILE] = found.astype(BF16).T

    wide = jnp.concatenate(
        [rows[f] for f in range(4)], axis=1
    )
    found = jnp.dot(wide, inverse[...], preferred_element_type=F32)
    solved[...] = found
    live[...] = found.astype(BF16)

    @pl.when((g == 0) & (p < 4))
    def _():
        for f in range(4):
            tile = lower[p * 4 + f]
            at = slice(f * TILE, (f + 1) * TILE)
            solved[:TILE, at] = tile
            live[:TILE, at] = jnp.where(f // 2 < p // 2, tile, 0.0).astype(BF16)

    @pl.when(g == 0)
    def _():
        for i, at in enumerate(chunks):
            pltpu.make_async_copy(arrived.at[at], held.at[at], landed.at[i]).wait()

    for pair in range(4):
        at = slice(pair * 256, (pair + 1) * 256)
        product = jnp.dot(live[...], factor_cols[:, at], preferred_element_type=F32)
        for t in range(3):
            for m in (pair * 2, pair * 2 + 1):
                down = slice(t * TILE, (t + 1) * TILE)
                across = slice(m * TILE, (m + 1) * TILE)
                total = front[down, across].astype(F32)
                for c in range(2):
                    slot = row_from[c * 24 + g * 3 + t] + col_from[c * 8 + m]
                    total = total + held[jnp.minimum(slot, ABSENT)].astype(F32)
                out[down, across] = total - product[down, (m % 2) * TILE : (m % 2 + 1) * TILE]

    for f in range(4):

        @pl.when(q == f)
        def _(f=f):
            out[:, :TILE] = solved[:, f * TILE : (f + 1) * TILE]


def finish(row_from, col_from, where, front, arrived, rows, cols, lower, inverse):
    return pl.pallas_call(
        finish_kernel,
        out_shape=jax.ShapeDtypeStruct((24 * TILE, 8 * TILE), F32),
        grid=(8,),
        in_specs=[
            spec(pltpu.SMEM),
            spec(pltpu.SMEM),
            spec(pltpu.SMEM),
            pl.BlockSpec((3 * TILE, 8 * TILE), lambda g: (g, 0)),
            spec(pl.ANY),
            pl.BlockSpec((4, 3 * TILE, TILE), lambda g: (0, g, 0)),
            spec(pltpu.VMEM),
            spec(pltpu.VMEM),
            spec(pltpu.VMEM),
        ],
        out_specs=pl.BlockSpec((3 * TILE, 8 * TILE), lambda g: (g, 0)),
        scratch_shapes=[
            pltpu.VMEM((4 * TILE, 8 * TILE), BF16),
            pltpu.VMEM((3 * TILE, 4 * TILE), F32),
            pltpu.VMEM((3 * TILE, 4 * TILE), BF16),
            pltpu.VMEM((ABSENT + 1, TILE, TILE), BF16),
            pltpu.SemaphoreType.DMA((8,)),
        ],
        compiler_params=pltpu.CompilerParams(vmem_limit_bytes=28 * 2**20),
        cost_estimate=pl.CostEstimate(flops=2**33, bytes_accessed=32 * 2**20, transcendentals=0),
        name="finish",
    )(row_from, col_from, where, front, arrived, rows, cols, lower, inverse)


def shards(front_block, child_blocks, row_offsets, tile_targets):
    where = jnp.stack([lax.axis_index("row"), lax.axis_index("col")]).astype(jnp.int32)
    picked = place(tile_targets, where, row_offsets, child_blocks)
    arrived = lax.all_to_all(
        picked.reshape(DEVICES, 2, TILE, TILE), ("row", "col"), 0, 0, tiled=True
    ).reshape(DEVICES * 2, TILE, TILE)
    row_from, col_from = index_tiles(tile_targets, where)
    column, heads = first_column(row_from, col_from, where, front_block, arrived)
    rows, cols, lower, inverse = spread_panels(
        column.reshape(COLS, 2, 96, TILE), heads
    )
    rows = rows.reshape(4, 24 * TILE, TILE)
    return finish(row_from, col_from, where, front_block, arrived, rows, cols, lower, inverse)


def solution(mesh):
    return jax.shard_map(
        shards,
        mesh=mesh,
        in_specs=(P("row", "col"), P(None, "row", "col"), P(), P()),
        out_specs=P("row", "col"),
        check_vma=False,
    )
```

```python
import jax
import jax.numpy as jnp
from jax import lax
from jax.experimental import pallas as pl
from jax.experimental.pallas import tpu as pltpu
from jax.sharding import PartitionSpec as P

TILE = 128
ROWS = 8
COLS = 16
DEVICES = ROWS * COLS
MESH = pl.DeviceIdType.MESH
BF16 = jnp.bfloat16
F32 = jnp.float32
NT = (((1,), (1,)), ((), ()))


def spec(space):
    return pl.BlockSpec(memory_space=space)


def iota(dim):
    return lax.broadcasted_iota(jnp.int32, (TILE, TILE), dim)


def one_hot(offsets):
    return jnp.where(iota(0) == offsets, 1.0, 0.0).astype(BF16)


def place_kernel(targets, where, offsets, child, picked, shifted, tiles, rank, seen, sent):
    c = pl.program_id(0)
    p = where[0]
    q = where[1]

    for d in range(ROWS):
        seen[d] = 0

    def order(l, carry):
        owner = lax.rem(targets[c, l * ROWS + p], ROWS)
        rank[l] = owner * COLS * 2 + seen[owner]
        seen[owner] = seen[owner] + 1
        return carry

    lax.fori_loop(0, 16, order, 0)

    def tile_offsets(t):
        both = offsets[:, pl.ds(pl.multiple_of(t * TILE, TILE), TILE)]
        return jnp.where(c == 0, both[:1], both[1:])

    for l in range(16):
        hot = one_hot(tile_offsets(l * ROWS + p))
        moved = jnp.dot(
            hot, child[0, l * TILE : (l + 1) * TILE, :], preferred_element_type=F32
        )
        shifted[l * TILE : (l + 1) * TILE, :] = moved.astype(BF16)
    for k in range(4):
        hot = one_hot(tile_offsets(k * COLS + q)).T
        front_col = targets[c, k * COLS + q]
        base = lax.rem(front_col, COLS) * 2
        for part in range(4):
            rows = shifted[part * 512 : (part + 1) * 512, k * TILE : (k + 1) * TILE]
            placed = jnp.dot(rows, hot, preferred_element_type=F32)
            for s in range(4):
                l = part * 4 + s
                tile = placed[s * TILE : (s + 1) * TILE]
                held = tiles.at[(c * 4 + k) * 16 + l]
                held[...] = tile.astype(BF16)
                pltpu.make_async_copy(held, picked.at[rank[l] + base], sent).start()

    @pl.when(c == 1)
    def _():
        pltpu.make_async_copy(tiles, tiles, sent).wait()


def place(targets, where, offsets, child):
    return pl.pallas_call(
        place_kernel,
        out_shape=jax.ShapeDtypeStruct((DEVICES * 2, TILE, TILE), BF16),
        grid=(2,),
        in_specs=[
            spec(pltpu.SMEM),
            spec(pltpu.SMEM),
            spec(pltpu.VMEM),
            pl.BlockSpec((1, 16 * TILE, 4 * TILE), lambda c: (c, 0, 0)),
        ],
        out_specs=spec(pl.ANY),
        scratch_shapes=[
            pltpu.VMEM((16 * TILE, 4 * TILE), BF16),
            pltpu.VMEM((DEVICES, TILE, TILE), BF16),
            pltpu.SMEM((16,), jnp.int32),
            pltpu.SMEM((ROWS,), jnp.int32),
            pltpu.SemaphoreType.DMA,
        ],
        compiler_params=pltpu.CompilerParams(vmem_limit_bytes=56 * 2**20),
        cost_estimate=pl.CostEstimate(flops=2**31, bytes_accessed=14 * 2**20, transcendentals=0),
        name="place",
    )(targets, where, offsets, child)


def mm(a, b):
    return jnp.dot(a, b, precision=lax.Precision.HIGHEST, preferred_element_type=F32)


def mm_nt(a, b):
    return lax.dot_general(
        a, b, NT, precision=lax.Precision.HIGHEST, preferred_element_type=F32
    )


def reciprocal(x):
    r = pl.reciprocal(x, approx=True)
    r = r * (2.0 - x * r)
    return r * (2.0 - x * r)


def lane(x, s):
    return jnp.take_along_axis(x, jnp.full((8, TILE), s, jnp.int32), axis=1)


def every(x, r):
    return jnp.broadcast_to(x[r : r + 1], (8, TILE))


def factor_tile(a):
    blocks = TILE // 8
    sub = lax.broadcasted_iota(jnp.int32, (8, TILE), 0)
    eye = jnp.where(iota(0) == iota(1), 1.0, 0.0)
    upper = [a[i * 8 : (i + 1) * 8] for i in range(blocks)]
    inverse = [eye[i * 8 : (i + 1) * 8] for i in range(blocks)]
    for s in range(0, TILE, 4):
        b, r = s // 8, s % 8
        c = [lane(upper[b], s + k) for k in range(4)]
        a00, a01, a02, a03 = (every(c[k], r) for k in range(4))
        a11, a12, a13 = (every(c[k], r + 1) for k in range(1, 4))
        a22, a23 = (every(c[k], r + 2) for k in range(2, 4))
        a33 = every(c[3], r + 3)
        det = reciprocal(a00 * a11 - a01 * a01)
        p00, p01, p11 = a11 * det, -a01 * det, a00 * det
        t20, t21 = a02 * p00 + a12 * p01, a02 * p01 + a12 * p11
        t30, t31 = a03 * p00 + a13 * p01, a03 * p01 + a13 * p11
        r22 = a22 - t20 * a02 - t21 * a12
        r23 = a23 - t20 * a03 - t21 * a13
        r33 = a33 - t30 * a03 - t31 * a13
        det = reciprocal(r22 * r33 - r23 * r23)
        i22, i23, i33 = r33 * det, -r23 * det, r22 * det
        ratio1 = a01 * reciprocal(a00)
        ratio3 = r23 * reciprocal(r22)
        for strips in (upper, inverse):
            u = [every(strips[b], r + k) for k in range(4)]
            l2 = u[2] - t20 * u[0] - t21 * u[1]
            l3 = u[3] - t30 * u[0] - t31 * u[1]
            w2 = i22 * l2 + i23 * l3
            w3 = i23 * l2 + i33 * l3
            w0 = p00 * u[0] + p01 * u[1] - t20 * w2 - t30 * w3
            w1 = p01 * u[0] + p11 * u[1] - t21 * w2 - t31 * w3
            one = strips[b]
            one = jnp.where(sub == r + 1, u[1] - ratio1 * u[0], one)
            one = jnp.where(sub == r + 2, l2, one)
            one = jnp.where(sub == r + 3, l3 - ratio3 * l2, one)
            if r == 0:
                after = strips[b] - c[0] * w0 - c[1] * w1 - c[2] * w2 - c[3] * w3
                one = jnp.where(sub > 3, after, one)
            if strips is upper:
                rows = [[lane(upper[i], s + k) for k in range(4)] for i in range(b + 1, blocks)]
            strips[b] = one
            for i in range(b + 1, blocks):
                e = rows[i - b - 1]
                strips[i] = strips[i] - e[0] * w0 - e[1] * w1 - e[2] * w2 - e[3] * w3
    u = jnp.concatenate(upper, axis=0)
    inv = jnp.concatenate(inverse, axis=0)
    diagonal = jnp.sum(jnp.where(iota(0) == iota(1), u, 0.0), axis=1, keepdims=True)
    root = lax.rsqrt(diagonal)
    u = jnp.where(iota(1) >= iota(0), u * root, 0.0)
    return u.T, inv * root


def factor_corner(early, corner, lower, inverse, work, inv, between, middle, after):
    def tile(i, j):
        return corner[j, i].astype(F32)

    one = early[...].astype(F32)
    work[0] = (one + one.T) * 0.5
    lower[...] = jnp.zeros_like(lower)

    def panel(j, carry):
        between(j)
        pivot, pivot_inv = factor_tile(work[j * 5])
        lower[j * 5] = pivot
        inv[j * 5] = pivot_inv

        @pl.when(j == 0)
        def _():
            middle()
            for i in range(1, 4):
                for k in range(i + 1):
                    one = tile(i, k)
                    work[i * 4 + k] = (one + tile(k, i).T) * 0.5 if i // 2 == k // 2 else one

        def solve(i, carry):
            lower[i * 4 + j] = mm_nt(work[i * 4 + j], pivot_inv)
            return carry

        lax.fori_loop(j + 1, 4, solve, 0)

        def update_row(i, carry):
            def update(k, carry):
                work[i * 4 + k] -= mm_nt(lower[i * 4 + j], lower[k * 4 + j])
                return carry

            return lax.fori_loop(j + 1, i + 1, update, carry)

        lax.fori_loop(j + 1, 4, update_row, 0)
        return carry

    lax.fori_loop(0, 4, panel, 0)
    after()
    inverse[...] = jnp.zeros_like(inverse)
    for j in range(4):
        column = {j: inv[j * 5]}
        for i in range(j + 1, 4):
            total = mm(lower[i * 4 + j], column[j])
            for k in range(j + 1, i):
                total = total + mm(lower[i * 4 + k], column[k])
            column[i] = -mm(inv[i * 5], total)
        for i in range(j, 4):
            block = column[i].T.astype(BF16)
            inverse[j * TILE : (j + 1) * TILE, i * TILE : (i + 1) * TILE] = block


ABSENT = DEVICES * 2


def index_kernel(targets, where, row_from, col_from, seen):
    p = where[0]
    q = where[1]

    def clear_rows(i, carry):
        row_from[i] = ABSENT
        return carry

    def clear_cols(i, carry):
        col_from[i] = ABSENT
        return carry

    lax.fori_loop(0, 48, clear_rows, 0)
    lax.fori_loop(0, 16, clear_cols, 0)
    for c in range(2):
        for d in range(ROWS):
            seen[d] = 0

        def visit_row(t, carry):
            goal = targets[c, t]

            @pl.when(lax.rem(goal, ROWS) == p)
            def _():
                source = lax.rem(t, ROWS)
                row_from[c * 24 + goal // ROWS] = source * COLS * 2 + seen[source]
                seen[source] = seen[source] + 1

            return carry

        lax.fori_loop(0, 128, visit_row, 0)

        def visit_col(t, carry):
            goal = targets[c, t]

            @pl.when(lax.rem(goal, COLS) == q)
            def _():
                col_from[c * 8 + goal // COLS] = lax.rem(t, COLS) * 2

            return carry

        lax.fori_loop(0, 64, visit_col, 0)


def index_tiles(targets, where):
    return pl.pallas_call(
        index_kernel,
        out_shape=(
            jax.ShapeDtypeStruct((48,), jnp.int32),
            jax.ShapeDtypeStruct((16,), jnp.int32),
        ),
        in_specs=[spec(pltpu.SMEM), spec(pltpu.SMEM)],
        out_specs=(spec(pltpu.SMEM), spec(pltpu.SMEM)),
        scratch_shapes=[pltpu.SMEM((ROWS,), jnp.int32)],
        cost_estimate=pl.CostEstimate(flops=2**20, bytes_accessed=2**16, transcendentals=0),
        name="index",
    )(targets, where)


def column_kernel(row_from, col_from, where, front, arrived, column, heads, held, landed):
    @pl.when(where[1] < 4)
    def _():
        slots = []
        for c in range(2):
            for l in range(24):
                i = c * 24 + l
                slot = row_from[i] + col_from[c * 8]
                slots.append(slot)

                @pl.when(slot < ABSENT)
                def _(i=i, slot=slot):
                    pltpu.make_async_copy(arrived.at[slot], held.at[i], landed.at[i]).start()

        for l in range(24):
            total = front[l * TILE : (l + 1) * TILE, :].astype(F32)
            for i in (l, 24 + l):

                @pl.when(slots[i] < ABSENT)
                def _(i=i):
                    pltpu.make_async_copy(held.at[i], held.at[i], landed.at[i]).wait()

                total = total + jnp.where(slots[i] < ABSENT, held[i].astype(F32), 0.0)
            column[l] = total.astype(BF16)
            if l < 16:
                heads[l % 2, l // 2] = total.astype(BF16)


def first_column(row_from, col_from, where, front, arrived):
    return pl.pallas_call(
        column_kernel,
        out_shape=(
            jax.ShapeDtypeStruct((24, TILE, TILE), BF16),
            jax.ShapeDtypeStruct((2, 8, TILE, TILE), BF16),
        ),
        grid=(1,),
        in_specs=[
            spec(pltpu.SMEM),
            spec(pltpu.SMEM),
            spec(pltpu.SMEM),
            pl.BlockSpec((24 * TILE, TILE), lambda i: (0, 0)),
            spec(pl.ANY),
        ],
        out_specs=(
            pl.BlockSpec((24, TILE, TILE), lambda i: (0, 0, 0)),
            pl.BlockSpec((2, 8, TILE, TILE), lambda i: (0, 0, 0, 0)),
        ),
        scratch_shapes=[
            pltpu.VMEM((48, TILE, TILE), BF16),
            pltpu.SemaphoreType.DMA((48,)),
        ],
        compiler_params=pltpu.CompilerParams(vmem_limit_bytes=52 * 2**20),
        cost_estimate=pl.CostEstimate(flops=2**20, bytes_accessed=2**22, transcendentals=0),
        name="column",
    )(row_from, col_from, where, front, arrived)


def spread_kernel(
    column,
    heads,
    rows,
    cols,
    lower,
    inverse,
    early,
    corner,
    work,
    inv,
    sends,
    recvs,
    share_sends,
    share_recvs,
    corner_sends,
    corner_recvs,
    head_sends,
    head_recvs,
    pass_sends,
    pass_recvs,
    early_sends,
    early_recvs,
    locals_,
):
    p = lax.axis_index("row")
    q = lax.axis_index("col")
    z, core = p // 2, lax.rem(p, 2)
    x, y = q // 4, lax.rem(q, 4)
    source = lax.rem(q, ROWS)
    hops = lax.rem(z + 4 - source // 2, 4)
    near = core == lax.rem(source, 2)
    sibling = (z * 2 + 1 - core, q)

    def at_x(d):
        return (p, lax.rem(x + d, 4) * 4 + y)

    def at_y(d):
        return (p, x * 4 + lax.rem(y + d, 4))

    def at_z(d):
        return (lax.rem(z + d, 4) * 2 + core, q)

    def at_row(d):
        return (lax.rem(p + d, ROWS), q)

    def at_col(d):
        return (p, lax.rem(q + d, COLS))

    barrier = pltpu.get_barrier_semaphore()
    for d in range(1, COLS):
        pl.semaphore_signal(barrier, inc=1, device_id=at_col(d), device_id_type=MESH)
    for d in range(1, ROWS):
        pl.semaphore_signal(barrier, inc=1, device_id=at_row(d), device_id_type=MESH)
    pl.semaphore_wait(barrier, COLS + ROWS - 2)

    def remote(src, dst, sent, landed, peer):
        return pltpu.make_async_remote_copy(
            src, dst, sent, landed, device_id=peer, device_id_type=MESH
        )

    def copy(part, slot, peer):
        return remote(part, part, sends.at[slot], recvs.at[slot], peer)

    def corner_copy(src, dst, sent, landed, peer):
        return remote(src, dst, corner_sends.at[sent], corner_recvs.at[landed], peer)

    def head_copy(h, f, peer):
        return remote(heads.at[h], cols.at[f], head_sends.at[h], head_recvs.at[f], peer)

    def share_copy(d):
        to = lax.rem(q + d, COLS)
        part = rows.at[y, to // 4, lax.rem(to, 4)]
        return remote(column.at[to], part, share_sends.at[d], share_recvs.at[y], at_col(d))

    def pass_copy(part, slot, peer):
        return remote(part, part, pass_sends.at[slot], pass_recvs.at[slot], peer)

    def own_copy(src, dst, slot):
        own = pltpu.make_async_copy(src, dst, locals_.at[slot])
        own.start()
        own.wait()

    def early_copy(src, sent, landed, peer):
        return remote(src, early, early_sends.at[sent], early_recvs.at[landed], peer)

    first_tile = heads.at[0, 0]

    @pl.when((p == 0) & (q == 0))
    def _():
        for d in range(1, ROWS):
            early_copy(first_tile, d - 1, 0, at_row(d)).start()
        own_copy(first_tile, early, 0)

    for r in range(4):

        @pl.when((q < 4) & (p == r))
        def _(r=r):
            for d in range(1, ROWS):
                corner_copy(first_tile, corner.at[y, r], d - 1, r, at_row(d)).start()
            own_copy(first_tile, corner.at[y, r], 0)

    @pl.when((p != 0) & (q == 0))
    def _():
        early_copy(early, 0, 0, at_row(1)).wait_recv()

    @pl.when(q == 0)
    def _():
        for d in (1, 2, 3):
            early_copy(early, 6 + d, d, at_x(d)).start()

    for r in range(4):

        @pl.when((q < 4) & (p != r))
        def _(r=r):
            corner_copy(first_tile, corner.at[y, r], 0, r, at_row(1)).wait_recv()

    @pl.when(x == 0)
    def _():
        for d in (1, 2, 3):
            corner_copy(corner.at[y], corner.at[y], 6 + d, 3 + d, at_x(d)).start()

    for d in (1, 2, 3):

        @pl.when((y == 0) & (x == d))
        def _(d=d):
            early_copy(early, 0, d, at_x(4 - d)).wait_recv()

    @pl.when(y == 0)
    def _():
        for d in (1, 2, 3):
            early_copy(early, 9 + d, 3 + d, at_y(d)).start()

    @pl.when((x == 0) & (q != p))
    def _():
        head_copy(0, y, (p, p)).start()

    @pl.when(x == 0)
    def _():
        head_copy(1, y, (p, p + 8)).start()

    @pl.when(x == 0)
    def _():
        for d in range(1, COLS):
            share_copy(d).start()
        own_copy(column.at[q], rows.at[y, 0, y], 1)

    @pl.when((x == 0) & (q == p))
    def _():
        own_copy(heads.at[0], cols.at[y], 2)

    for d in (1, 2, 3):

        @pl.when(x == d)
        def _(d=d):
            corner_copy(corner.at[y], corner.at[y], 6 + d, 3 + d, at_x(4 - d)).wait_recv()

    last = [corner_copy(corner.at[y], corner.at[y], 9 + d, 6 + d, at_y(d)) for d in (1, 2, 3)]
    for one in last:
        one.start()

    for d in (1, 2, 3):

        @pl.when(y == d)
        def _(d=d):
            early_copy(early, 0, 3 + d, at_y(4 - d)).wait_recv()

    first = []
    for d in (1, 2, 3):
        first.append(copy(rows.at[:, x, y, 0], d - 1, at_x(d)))
        first.append(copy(rows.at[:, x, y, 1], d + 2, at_y(d)))
    second = []
    for d in (1, 2, 3):
        second.append(copy(rows.at[:, :, y, 0], d + 5, at_y(d)))
        second.append(copy(rows.at[:, x, :, 1], d + 8, at_x(d)))
    low, high = cols.at[pl.ds(0, 2)], cols.at[pl.ds(2, 2)]

    def middle():
        for f in range(4):

            @pl.when(q != f)
            def _(f=f):
                part = rows.at[f, x, y]
                remote(part, part, share_sends.at[0], share_recvs.at[f], at_col(1)).wait_recv()

        for one in first:
            one.start()

        for one in last:
            one.wait_recv()

    def between(j):
        @pl.when(j == 1)
        def _():
            for one in first:
                one.wait_recv()
            for one in second:
                one.start()

        for f in range(4):

            @pl.when((j == 1) & (p == source) & (q != f))
            def _(f=f):
                head_copy(0, f, (p, p)).wait_recv()

        @pl.when((j == 1) & (p == source))
        def _():
            pass_copy(low, 0, at_z(1)).start()
            pass_copy(high, 1, at_z(3)).start()
            pass_copy(high, 2, at_z(1)).start()
            pass_copy(low, 3, at_z(3)).start()
            pass_copy(cols, 6, sibling).start()

        @pl.when((j == 3) & near & (hops == 1))
        def _():
            pass_copy(low, 0, at_z(3)).wait_recv()
            pass_copy(low, 4, at_z(1)).start()
            pass_copy(high, 2, at_z(3)).wait_recv()
            pass_copy(cols, 6, sibling).start()

        @pl.when((j == 3) & near & (hops == 3))
        def _():
            pass_copy(high, 1, at_z(1)).wait_recv()
            pass_copy(high, 5, at_z(3)).start()
            pass_copy(low, 3, at_z(1)).wait_recv()
            pass_copy(cols, 6, sibling).start()

    def after():
        @pl.when(near & (hops == 2))
        def _():
            pass_copy(low, 4, at_z(3)).wait_recv()
            pass_copy(high, 5, at_z(1)).wait_recv()
            pass_copy(cols, 6, sibling).start()

    factor_corner(early, corner, lower, inverse, work, inv, between, middle, after)

    for one in second:
        one.wait_recv()

    @pl.when(jnp.logical_not(near))
    def _():
        pass_copy(cols, 6, sibling).wait_recv()

    @pl.when(near)
    def _():
        pass_copy(cols, 6, sibling).wait_send()

    @pl.when(p == source)
    def _():
        pass_copy(low, 0, at_z(1)).wait_send()
        pass_copy(high, 1, at_z(3)).wait_send()
        pass_copy(high, 2, at_z(1)).wait_send()
        pass_copy(low, 3, at_z(3)).wait_send()

    @pl.when(near & (hops == 1))
    def _():
        pass_copy(low, 4, at_z(1)).wait_send()

    @pl.when(near & (hops == 3))
    def _():
        pass_copy(high, 5, at_z(3)).wait_send()

    for one in last + first + second:
        one.wait_send()

    @pl.when(x == 0)
    def _():
        for d in range(1, COLS):
            share_copy(d).wait_send()
        for d in (1, 2, 3):
            corner_copy(corner.at[y], corner.at[y], 6 + d, 3 + d, at_x(d)).wait_send()
        head_copy(1, y, (p, p + 8)).wait_send()

    @pl.when((x == 0) & (q != p))
    def _():
        head_copy(0, y, (p, p)).wait_send()

    @pl.when((q < 4) & (p < 4))
    def _():
        for d in range(1, ROWS):
            corner_copy(first_tile, early, d - 1, 0, at_row(d)).wait_send()

    @pl.when((p == 0) & (q == 0))
    def _():
        for d in range(1, ROWS):
            early_copy(first_tile, d - 1, 0, at_row(d)).wait_send()

    @pl.when(q == 0)
    def _():
        for d in (1, 2, 3):
            early_copy(early, 6 + d, d, at_x(d)).wait_send()

    @pl.when(y == 0)
    def _():
        for d in (1, 2, 3):
            early_copy(early, 9 + d, 3 + d, at_y(d)).wait_send()


def spread_panels(column, heads):
    return pl.pallas_call(
        spread_kernel,
        out_shape=(
            jax.ShapeDtypeStruct((4, 4, 4, 2, 96, TILE), BF16),
            jax.ShapeDtypeStruct((4, 8, TILE, TILE), BF16),
            jax.ShapeDtypeStruct((16, TILE, TILE), F32),
            jax.ShapeDtypeStruct((4 * TILE, 4 * TILE), BF16),
        ),
        in_specs=[spec(pltpu.VMEM)] * 2,
        out_specs=(spec(pltpu.VMEM),) * 4,
        scratch_shapes=[
            pltpu.VMEM((TILE, TILE), BF16),
            pltpu.VMEM((4, 4, TILE, TILE), BF16),
            pltpu.VMEM((16, TILE, TILE), F32),
            pltpu.VMEM((16, TILE, TILE), F32),
            pltpu.SemaphoreType.DMA((12,)),
            pltpu.SemaphoreType.DMA((12,)),
            pltpu.SemaphoreType.DMA((COLS,)),
            pltpu.SemaphoreType.DMA((4,)),
            pltpu.SemaphoreType.DMA((13,)),
            pltpu.SemaphoreType.DMA((10,)),
            pltpu.SemaphoreType.DMA((2,)),
            pltpu.SemaphoreType.DMA((4,)),
            pltpu.SemaphoreType.DMA((7,)),
            pltpu.SemaphoreType.DMA((7,)),
            pltpu.SemaphoreType.DMA((13,)),
            pltpu.SemaphoreType.DMA((7,)),
            pltpu.SemaphoreType.DMA((3,)),
        ],
        compiler_params=pltpu.CompilerParams(
            collective_id=2, has_side_effects=True, vmem_limit_bytes=20 * 2**20
        ),
        cost_estimate=pl.CostEstimate(flops=2**30, bytes_accessed=2**23, transcendentals=0),
        name="spread",
    )(column, heads)


def finish_kernel(
    row_from,
    col_from,
    where,
    front,
    arrived,
    rows,
    cols,
    lower,
    inverse,
    out,
    factor_cols,
    solved,
    live,
    held,
    landed,
):
    g = pl.program_id(0)
    p = where[0]
    q = where[1]
    chunks = [pl.ds(i * 32, 32) for i in range(8)]

    @pl.when(g == 0)
    def _():
        for i, at in enumerate(chunks):
            pltpu.make_async_copy(arrived.at[at], held.at[at], landed.at[i]).start()
        held[ABSENT] = jnp.zeros((TILE, TILE), BF16)
        for m in range(8):
            wide = jnp.concatenate([cols[f, m] for f in range(4)], axis=1)
            found = jnp.dot(wide, inverse[...], preferred_element_type=F32)
            factor_cols[:, m * TILE : (m + 1) * TILE] = found.astype(BF16).T

    wide = jnp.concatenate(
        [rows[f] for f in range(4)], axis=1
    )
    found = jnp.dot(wide, inverse[...], preferred_element_type=F32)
    solved[...] = found
    live[...] = found.astype(BF16)

    @pl.when((g == 0) & (p < 4))
    def _():
        for f in range(4):
            tile = lower[p * 4 + f]
            at = slice(f * TILE, (f + 1) * TILE)
            solved[:TILE, at] = tile
            live[:TILE, at] = jnp.where(f // 2 < p // 2, tile, 0.0).astype(BF16)

    @pl.when(g == 0)
    def _():
        for i, at in enumerate(chunks):
            pltpu.make_async_copy(arrived.at[at], held.at[at], landed.at[i]).wait()

    for pair in range(4):
        at = slice(pair * 256, (pair + 1) * 256)
        product = jnp.dot(live[...], factor_cols[:, at], preferred_element_type=F32)
        for t in range(3):
            for m in (pair * 2, pair * 2 + 1):
                down = slice(t * TILE, (t + 1) * TILE)
                across = slice(m * TILE, (m + 1) * TILE)
                total = front[down, across].astype(F32)
                for c in range(2):
                    slot = row_from[c * 24 + g * 3 + t] + col_from[c * 8 + m]
                    total = total + held[jnp.minimum(slot, ABSENT)].astype(F32)
                out[down, across] = total - product[down, (m % 2) * TILE : (m % 2 + 1) * TILE]

    for f in range(4):

        @pl.when(q == f)
        def _(f=f):
            out[:, :TILE] = solved[:, f * TILE : (f + 1) * TILE]


def finish(row_from, col_from, where, front, arrived, rows, cols, lower, inverse):
    return pl.pallas_call(
        finish_kernel,
        out_shape=jax.ShapeDtypeStruct((24 * TILE, 8 * TILE), F32),
        grid=(8,),
        in_specs=[
            spec(pltpu.SMEM),
            spec(pltpu.SMEM),
            spec(pltpu.SMEM),
            pl.BlockSpec((3 * TILE, 8 * TILE), lambda g: (g, 0)),
            spec(pl.ANY),
            pl.BlockSpec((4, 3 * TILE, TILE), lambda g: (0, g, 0)),
            spec(pltpu.VMEM),
            spec(pltpu.VMEM),
            spec(pltpu.VMEM),
        ],
        out_specs=pl.BlockSpec((3 * TILE, 8 * TILE), lambda g: (g, 0)),
        scratch_shapes=[
            pltpu.VMEM((4 * TILE, 8 * TILE), BF16),
            pltpu.VMEM((3 * TILE, 4 * TILE), F32),
            pltpu.VMEM((3 * TILE, 4 * TILE), BF16),
            pltpu.VMEM((ABSENT + 1, TILE, TILE), BF16),
            pltpu.SemaphoreType.DMA((8,)),
        ],
        compiler_params=pltpu.CompilerParams(vmem_limit_bytes=28 * 2**20),
        cost_estimate=pl.CostEstimate(flops=2**33, bytes_accessed=32 * 2**20, transcendentals=0),
        name="finish",
    )(row_from, col_from, where, front, arrived, rows, cols, lower, inverse)


def shards(front_block, child_blocks, row_offsets, tile_targets):
    where = jnp.stack([lax.axis_index("row"), lax.axis_index("col")]).astype(jnp.int32)
    picked = place(tile_targets, where, row_offsets, child_blocks)
    arrived = lax.all_to_all(
        picked.reshape(DEVICES, 2, TILE, TILE), ("row", "col"), 0, 0, tiled=True
    ).reshape(DEVICES * 2, TILE, TILE)
    row_from, col_from = index_tiles(tile_targets, where)
    column, heads = first_column(row_from, col_from, where, front_block, arrived)
    rows, cols, lower, inverse = spread_panels(
        column.reshape(COLS, 2, 96, TILE), heads
    )
    rows = rows.reshape(4, 24 * TILE, TILE)
    return finish(row_from, col_from, where, front_block, arrived, rows, cols, lower, inverse)


def solution(mesh):
    return jax.shard_map(
        shards,
        mesh=mesh,
        in_specs=(P("row", "col"), P(None, "row", "col"), P(), P()),
        out_specs=P("row", "col"),
        check_vma=False,
    )
```
